32 devices in a mesh: set: 8 (over z, core), col: 4 (over y, x).
Axes of the slice: x: 2, y: 2, z: 4, core: 2. Of those that a mesh axis runs over, the one named last changes fastest.
Arguments:
- factor: float32 [8, 2, 131072], P('col'), may hold values from -8 to 8
- velocity: float32 [8, 2, 131072], P(None, None, ('set', 'col')), may hold values from -4 to 4
- labels: int32 [8, 17], P('set'), may hold values from 0 to 2
- counts: int32 [8, 131072], P('set'), may hold values from 1 to 28, as said below
Outputs:
- new_factor: float32 [8, 2, 131072], P(None, None, ('set', 'col'))
- new_velocity: float32 [8, 2, 131072], P(None, None, ('set', 'col'))
The draws below stay inside these ranges and needn't reach their ends.
Inputs may be any that keep to these rules, and one draw needn't show every extreme that they name: `labels`: 0 selects the X basis, 1 the Y basis, 2 the Z basis. The counts of setting s lie between 1 and 4 + (24 s) // 7.
All inputs are finite; a program needn't handle non-finite values.
Results may differ from the reference program's by a relative error of at most 0.0003.
Values sent between devices are 32-bit elements; how exact they have to be, the bound alone decides.
A program may use at most 64 MiB of HBM per device.

```python
import jax
import jax.numpy as jnp
from jax import lax

QA = 8
QB = 9
QUBITS = 17
ORDER = 131072
RANK = 8
SETTINGS = 8


def draw_factor(key, part):
    base = jax.random.fold_in(key, 11)
    key_own, key_common = jax.random.split(base, 2)
    own = jax.random.normal(key_own, (RANK, 2, ORDER), jnp.float32)
    common = jax.random.normal(key_common, (1, 2, ORDER), jnp.float32)
    values = own + 0.5 * common
    return jnp.clip(values, -8.0, 8.0)


def draw_counts(key, part):
    base = jax.random.fold_in(key, 23)
    setting_index = jnp.arange(SETTINGS, dtype=jnp.int32)
    upper = 4 + 24 * setting_index // (SETTINGS - 1)
    return jax.random.randint(base, (SETTINGS, ORDER), 1, upper[:, None] + 1, jnp.int32)


def plant(drawn, key, low, largest):
    place = [jax.random.randint(jax.random.fold_in(key, axis), (), 0, length) for axis, length in enumerate(drawn.shape)]
    widest = drawn.shape.index(max(drawn.shape))
    neighbour = place[:widest] + [(place[widest] + 1) % drawn.shape[widest]] + place[widest + 1:]
    return drawn.at[tuple(place)].set(low).at[tuple(neighbour)].set(largest)


def level_of(stream_key, extent, cuts, low, top_value):
    def one(axis_at, shards_of):
        draws = jax.random.uniform(jax.random.fold_in(jax.random.fold_in(stream_key, 6), axis_at), (shards_of,), jnp.float32, low / len(cuts), top_value / len(cuts))
        return jnp.repeat(jnp.exp(draws), extent[axis_at] // shards_of).reshape((-1,) + (1,) * (len(extent) - axis_at - 1))

    loudness = one(*cuts[0])
    for cut in cuts[1:]:
        loudness = loudness * one(*cut)
    return loudness


def noise(stream_key, extent, spread, bound, shards=(), kind=jnp.bfloat16):
    values = spread * jax.random.normal(stream_key, extent, jnp.float32)
    if shards:
        values = values * level_of(stream_key, extent, shards, -0.22, 0.18)
    return jnp.clip(values, -bound, bound).astype(kind)


def setup_inputs(seed: int = 0) -> dict:
    arg_keys = jax.random.split(jax.random.key(seed), 5)
    return {
        "factor": draw_factor(jax.random.fold_in(arg_keys[4], 71), 0),
        "velocity": noise(arg_keys[1], (RANK, 2, ORDER), 0.5, 4.0, ((2, 32),), jnp.float32),
        "labels": plant(jax.random.randint(arg_keys[2], (SETTINGS, QUBITS), 0, 3), jax.random.fold_in(arg_keys[2], 1), 0, 2).astype(jnp.int32),
        "counts": draw_counts(jax.random.fold_in(arg_keys[4], 71), 0),
    }


mixing = 0.1
penalty = 8.0
momentum = 0.9
step_size = 0.5
half_root = 0.7071067811865476
count_norm = 8.0


def kron_factor(labels_part):
    width = labels_part.shape[0]
    size = 2 ** width
    row_index = lax.broadcasted_iota(jnp.int32, (size, size), 0)
    col_index = lax.broadcasted_iota(jnp.int32, (size, size), 1)
    phase = jnp.zeros((size, size), jnp.int32)
    allowed = jnp.ones((size, size), jnp.bool_)
    nonz_count = jnp.zeros((), jnp.float32)
    for position in range(width):
        shift_amount = width - 1 - position
        row_bit = (row_index >> shift_amount) & 1
        col_bit = (col_index >> shift_amount) & 1
        label_value = labels_part[position]
        phase = phase + jnp.where(label_value == 0, 2 * row_bit * col_bit, jnp.where(label_value == 1, col_bit * (3 + 2 * row_bit), 0))
        allowed = jnp.logical_and(allowed, jnp.logical_or(label_value != 2, row_bit == col_bit))
        nonz_count = nonz_count + jnp.where(label_value == 2, 0.0, 1.0).astype(jnp.float32)
    phase = phase % 4
    magnitude = jnp.power(jnp.float32(half_root), nonz_count)
    scale = jnp.where(allowed, magnitude, jnp.float32(0.0))
    mat_real = jnp.where(phase == 0, 1.0, jnp.where(phase == 2, -1.0, 0.0)).astype(jnp.float32) * scale
    mat_imag = jnp.where(phase == 1, 1.0, jnp.where(phase == 3, -1.0, 0.0)).astype(jnp.float32) * scale
    return mat_real, mat_imag


def setting_forms(labels_row):
    left_real, left_imag = kron_factor(labels_row[:QA])
    right_real, right_imag = kron_factor(labels_row[QA:])
    return left_real, left_imag, right_real, right_imag


def rotate_forward(columns, forms):
    left_real, left_imag, right_real, right_imag = forms
    high = lax.Precision.HIGHEST
    first_real = jnp.einsum('ae,rceb->rcab', left_real, columns, precision=high)
    first_imag = jnp.einsum('ae,rceb->rcab', left_imag, columns, precision=high)
    section_one = jnp.stack([first_real[:, 0] - first_imag[:, 1], first_real[:, 1] + first_imag[:, 0]], axis=1)
    second_real = jnp.einsum('rcab,db->rcad', section_one, right_real, precision=high)
    second_imag = jnp.einsum('rcab,db->rcad', section_one, right_imag, precision=high)
    return jnp.stack([second_real[:, 0] - second_imag[:, 1], second_real[:, 1] + second_imag[:, 0]], axis=1)


def rotate_back(columns, forms):
    left_real, left_imag, right_real, right_imag = forms
    high = lax.Precision.HIGHEST
    first_real = jnp.einsum('rcad,db->rcab', columns, right_real, precision=high)
    first_imag = jnp.einsum('rcad,db->rcab', columns, right_imag, precision=high)
    section_one = jnp.stack([first_real[:, 0] + first_imag[:, 1], first_real[:, 1] - first_imag[:, 0]], axis=1)
    second_real = jnp.einsum('ae,rcab->rceb', left_real, section_one, precision=high)
    second_imag = jnp.einsum('ae,rcab->rceb', left_imag, section_one, precision=high)
    return jnp.stack([second_real[:, 0] + second_imag[:, 1], second_real[:, 1] - second_imag[:, 0]], axis=1)


def reference(factor, velocity, labels, counts):
    left_size = 2 ** QA
    right_size = 2 ** QB
    columns = factor.reshape(RANK, 2, left_size, right_size)
    trace_value = jnp.sum(factor * factor)

    def per_setting(carry, inputs):
        adjoint_sum, ratio_sum = carry
        labels_row, counts_row = inputs
        forms = setting_forms(labels_row)
        rotated = rotate_forward(columns, forms)
        probability = jnp.sum(rotated * rotated, axis=(0, 1)).reshape(ORDER)
        quasi = (1.0 - mixing) * probability / trace_value + mixing / ORDER
        weights = counts_row.astype(jnp.float32) / ((count_norm * ORDER) * quasi)
        ratio_sum = ratio_sum + jnp.sum(weights * probability) / trace_value
        weighted = rotated * weights.reshape(1, 1, left_size, right_size)
        adjoint_sum = adjoint_sum + rotate_back(weighted, forms)
        return (adjoint_sum, ratio_sum), None

    start = (jnp.zeros((RANK, 2, left_size, right_size), jnp.float32), jnp.zeros((), jnp.float32))
    (adjoint_sum, ratio_total), unused = lax.scan(per_setting, start, (labels, counts))
    adjoint_sum = adjoint_sum.reshape(RANK, 2, ORDER)
    block_real = factor[:, 0]
    block_imag = factor[:, 1]
    high = lax.Precision.HIGHEST
    gram_real = jnp.dot(block_real, block_real.T, precision=high) + jnp.dot(block_imag, block_imag.T, precision=high)
    gram_imag = jnp.dot(block_real, block_imag.T, precision=high) - jnp.dot(block_imag, block_real.T, precision=high)
    purity = (jnp.sum(jnp.square(gram_real)) + jnp.sum(jnp.square(gram_imag))) / jnp.square(trace_value)
    mixed_real = jnp.dot(gram_real.T, block_real, precision=high) - jnp.dot(gram_imag.T, block_imag, precision=high)
    mixed_imag = jnp.dot(gram_real.T, block_imag, precision=high) + jnp.dot(gram_imag.T, block_real, precision=high)
    mixed = jnp.stack([mixed_real, mixed_imag], axis=1)
    gradient = -((1.0 - mixing) / SETTINGS) * (adjoint_sum - ratio_total * factor) + penalty * (2.0 * mixed / trace_value - 2.0 * purity * factor)
    new_velocity = momentum * velocity + gradient
    new_factor = factor - step_size * new_velocity
    return new_factor, new_velocity
```

```python
import functools

import jax
import jax.numpy as jnp
from jax import lax
from jax.experimental import pallas as pl
from jax.experimental.pallas import tpu as pltpu
from jax.sharding import PartitionSpec as P

QA = 8
QB = 9
LANES = 128

mixing = 0.1
penalty = 8.0
momentum = 0.9
step_size = 0.5
count_norm = 8.0
MESH = pl.DeviceIdType.MESH


def fold_parity(x):
    x = x ^ (x >> 8)
    x = x ^ (x >> 4)
    x = x ^ (x >> 2)
    x = x ^ (x >> 1)
    return x & 1


def bit_count(x):
    x = x - ((x >> 1) & 0x55555)
    x = (x & 0x33333) + ((x >> 2) & 0x33333)
    x = (x + (x >> 4)) & 0xF0F0F
    return (x + (x >> 8) + (x >> 16)) & 0xFF


def sign_matrix(mask, size):
    row = lax.broadcasted_iota(jnp.int32, (size, size), 0)
    col = lax.broadcasted_iota(jnp.int32, (size, size), 1)
    sign = 1 - 2 * fold_parity(row & col & mask)
    keep = ((row ^ col) & (mask ^ (size - 1))) == 0
    return jnp.where(keep, sign, 0).astype(jnp.float32).astype(jnp.bfloat16)


def split(x):
    high = x.astype(jnp.bfloat16)
    return high, (x - high.astype(jnp.float32)).astype(jnp.bfloat16)


def dot(a, b):
    return jnp.dot(a, b, preferred_element_type=jnp.float32)


def kernel(n_set, n_col, labels, factor, velocity, counts, out_factor, out_velocity,
           hb, high, low, g, y, psend, precv, wown, wrecv, fb, sw, ab, stat, stat_col, stat_sum, stat_all,
           xbuf, right_buf, left_buf,
           f_send, f_recv, p_send, p_recv, w_send, w_recv, c_send, c_recv, s_send, s_recv,
           x_send, x_recv, r_send, r_recv, l_send, l_recv, a_send, a_recv):
    rank = factor.shape[0]
    left, rsize = 2**QA, 2**QB
    order = left * rsize
    tiles = rsize // LANES
    total = n_col * rank
    chunk = left // n_col
    block = factor.shape[1] // n_set
    part = block // n_col
    zs = n_set // 2
    i = lax.axis_index("set")
    j = lax.axis_index("col")
    z, core = i // 2, i % 2

    def col_peer(s):
        return lax.rem(j + s, n_col)

    def set_peer(s):
        return lax.rem(i + s, n_set)

    def rows_of(index, size):
        return pl.ds(pl.multiple_of(index * size, size), size)

    barrier = pltpu.get_barrier_semaphore()
    for s in range(1, n_col):
        pl.semaphore_signal(barrier, inc=1, device_id=(i, col_peer(s)), device_id_type=MESH)
    for s in range(1, n_set):
        pl.semaphore_signal(barrier, inc=1, device_id=(set_peer(s), j), device_id_type=MESH)
    pl.semaphore_wait(barrier, n_col - 1 + n_set - 1)

    def copy(src, dst, send, recv, where):
        return pltpu.make_async_remote_copy(
            src_ref=src, dst_ref=dst, send_sem=send, recv_sem=recv, device_id=where, device_id_type=MESH)

    mine = pl.ds(j * rank, rank)
    f_copies = []
    for s in range(1, n_col):
        peer = col_peer(s)
        f_copies.append(copy(factor.at[:, rows_of(i * n_col + peer, part)], fb.at[mine],
                             f_send.at[s], f_recv.at[s], (i, peer)))
        f_copies[-1].start()

    nonz = jnp.int32(0)
    ymask = jnp.int32(0)
    scale = jnp.float32(1.0)
    for q in range(QA + QB):
        label = labels[0, q]
        bit = 1 << (QA + QB - 1 - q)
        nonz = nonz + jnp.where(label == 2, 0, bit)
        ymask = ymask + jnp.where(label == 1, bit, 0)
        scale = scale * jnp.where(label == 2, 1.0, 0.5).astype(jnp.float32)
    ha = sign_matrix(nonz >> QB, left)
    hb[...] = sign_matrix(nonz & (rsize - 1), rsize)

    index = (lax.broadcasted_iota(jnp.int32, (left, LANES), 0) * rsize
             + lax.broadcasted_iota(jnp.int32, (left, LANES), 1))

    def phases(b):
        phase = bit_count((index + b * LANES) & ymask) & 3
        odd = (phase & 1) == 1
        late = (1 - 2 * (phase >> 1)).astype(jnp.float32)
        mid = (1 - 2 * ((phase ^ (phase >> 1)) & 1)).astype(jnp.float32)
        return odd, late, mid

    square = jnp.zeros((left, LANES), jnp.float32)
    for b in range(tiles):
        odd, late, mid = phases(b)
        lanes = slice(b * LANES, (b + 1) * LANES)
        for r in range(rank):
            re = factor[r, pl.ds(2 * b, left, stride=2 * tiles), :]
            im = factor[r, pl.ds(2 * b + 1, left, stride=2 * tiles), :]
            square = square + re * re + im * im
            for c, x in enumerate((jnp.where(odd, im, re) * late, jnp.where(odd, re, im) * mid)):
                xh, xl = split(x)
                high[2 * r + c, :, lanes] = xh
                low[2 * r + c, :, lanes] = xl
    for rc in range(2 * rank):
        first = dot(ha, high[rc]) + dot(ha, low[rc])
        xh, xl = split(first)
        high[rc] = xh
        low[rc] = xl
    trace_part = jnp.sum(jnp.sum(square, axis=0, keepdims=True), axis=1, keepdims=True)

    p_copies = []
    for s in list(range(1, n_col)) + [0]:
        peer = col_peer(s)
        rows = rows_of(peer, chunk)
        xh = high[:, rows, :].reshape(2 * rank * chunk, rsize)
        xl = low[:, rows, :].reshape(2 * rank * chunk, rsize)
        second = (dot(xh, hb[...]) + dot(xl, hb[...])).reshape(2 * rank, chunk, rsize)
        g[:, rows, :] = second
        psend[s, :chunk, :] = scale * jnp.sum(second * second, axis=0)
        psend[s, chunk:, :] = jnp.broadcast_to(trace_part, (8, rsize))
        if s:
            p_copies.append(copy(psend.at[s], precv.at[s], p_send.at[s], p_recv.at[s], (i, peer)))
            p_copies[-1].start()

    for r in range(rank):
        fb[j * rank + r] = factor[r, rows_of(i * n_col + j, part), :]
    for c in f_copies:
        c.wait()
    every = fb[...].reshape(total * part, LANES)
    parity = lax.broadcasted_iota(jnp.int32, every.shape, 0) & 1
    swapped = jnp.where(parity == 0, pltpu.roll(every, total * part - 1, 0), -pltpu.roll(every, 1, 0))
    sw[...] = swapped.reshape(total, part, LANES)
    lane = lax.broadcasted_iota(jnp.int32, (total, LANES), 1)
    gram = jnp.zeros((total, LANES), jnp.float32)
    for b in range(total):
        real = jnp.sum(jnp.sum(fb[...] * fb[b][None], axis=1), axis=1, keepdims=True)
        imag = jnp.sum(jnp.sum(fb[...] * sw[b][None], axis=1), axis=1, keepdims=True)
        gram = jnp.where(lane == b, real, gram)
        gram = jnp.where(lane == LANES // 2 + b, imag, gram)
    stat[8:, :] = gram

    prob = psend[0]
    for s, c in enumerate(p_copies, 1):
        c.wait()
        prob = prob + precv[s]
    trace_value = prob[chunk : chunk + 1, :1]
    prob = prob[:chunk]
    quasi = (1.0 - mixing) * prob / trace_value + mixing / order
    count = jnp.concatenate(
        [counts[pl.ds(j * (chunk * tiles) + b, chunk, stride=tiles), :] for b in range(tiles)], axis=1
    ).astype(jnp.float32)
    weight = count / (count_norm * order * quasi)
    wown[...] = weight
    ratio = jnp.sum((weight * prob / trace_value).reshape(chunk // 8, 8, rsize), axis=0)
    folded = ratio[:, :LANES]
    for b in range(1, tiles):
        folded = folded + ratio[:, b * LANES : (b + 1) * LANES]
    stat[:8, :] = folded
    w_copies, c_copies = [], []
    for s in range(1, n_col):
        where = (i, col_peer(s))
        w_copies.append(copy(wown, wrecv.at[s], w_send.at[s], w_recv.at[s], where))
        w_copies[-1].start()
        c_copies.append(copy(stat, stat_col.at[s], c_send.at[s], c_recv.at[s], where))
        c_copies[-1].start()

    for s in range(n_col):
        if s:
            w_copies[s - 1].wait()
            weight = wrecv[s]
        else:
            weight = wown[...]
        rows = rows_of(lax.rem(j - s + n_col, n_col), chunk)
        xh, xl = split((g[:, rows, :] * (weight * scale)[None]).reshape(2 * rank * chunk, rsize))
        xh, xl = split(dot(xh, hb[...]) + dot(xl, hb[...]))
        high[:, rows, :] = xh.reshape(2 * rank, chunk, rsize)
        low[:, rows, :] = xl.reshape(2 * rank, chunk, rsize)

    summed = stat[...]
    for s, c in enumerate(c_copies, 1):
        c.wait()
        summed = summed + stat_col[s]
    stat_sum[...] = summed
    s_copies = []
    for s in range(1, n_set):
        s_copies.append(copy(stat_sum, stat_all.at[s], s_send.at[s], s_recv.at[s], (set_peer(s), j)))
        s_copies[-1].start()

    odd_late_mid = [phases(b) for b in range(tiles)]
    for r in range(rank):
        re_all = dot(ha, high[2 * r]) + dot(ha, low[2 * r])
        im_all = dot(ha, high[2 * r + 1]) + dot(ha, low[2 * r + 1])
        for b in range(tiles):
            odd, late, mid = odd_late_mid[b]
            re = re_all[:, b * LANES : (b + 1) * LANES]
            im = im_all[:, b * LANES : (b + 1) * LANES]
            y[r, pl.ds(2 * b, left, stride=2 * tiles), :] = jnp.where(odd, im, re) * mid
            y[r, pl.ds(2 * b + 1, left, stride=2 * tiles), :] = jnp.where(odd, re, im) * late

    def rows_for(d, side):
        return rows_of(2 * d + side, block)

    def across(r, d):
        return copy(y.at[r, rows_for(d, 1 - core)], xbuf.at[d, r], x_send.at[d, r], x_recv.at[d, r],
                    (2 * z + 1 - core, j))

    def rightward(r, d):
        return copy(y.at[r, rows_for(d, core)], right_buf.at[d, r], r_send.at[d, r], r_recv.at[d, r],
                    (lax.rem(i + 2, n_set), j))

    def leftward(r, d):
        return copy(y.at[r, rows_for(d, core)], left_buf.at[d, r], l_send.at[d, r], l_recv.at[d, r],
                    (lax.rem(i + n_set - 2, n_set), j))

    for t in range(zs):
        for r in range(rank):
            across(r, lax.rem(z + t + 1, zs)).start()
    for t in range(zs - 1):
        for r in range(rank):
            @pl.when(t >= z)
            def _():
                d = z + zs - 1 - t
                across(r, d).wait_recv()
                y[r, rows_for(d, core), :] += xbuf[d, r]

                @pl.when(z > 0)
                def _():
                    rightward(r, d).wait_recv()
                    y[r, rows_for(d, core), :] += right_buf[d, r]

                rightward(r, d).start()

            @pl.when(t >= zs - 1 - z)
            def _():
                d = t - (zs - 1 - z)
                across(r, d).wait_recv()
                y[r, rows_for(d, core), :] += xbuf[d, r]

                @pl.when(z < zs - 1)
                def _():
                    leftward(r, d).wait_recv()
                    y[r, rows_for(d, core), :] += left_buf[d, r]

                leftward(r, d).start()

    summed = stat_sum[...]
    for s, c in enumerate(s_copies, 1):
        c.wait()
        summed = summed + stat_all[s]
    ratio_total = jnp.sum(jnp.sum(summed[:8], axis=0, keepdims=True), axis=1, keepdims=True)
    gram = summed[8:]
    purity = jnp.sum(jnp.sum(gram * gram, axis=0, keepdims=True), axis=1, keepdims=True) / (trace_value * trace_value)
    settings_all = n_set * labels.shape[0]
    rate = (1.0 - mixing) / settings_all
    own = rate * ratio_total - 2.0 * penalty * purity
    for b in range(total):
        mixed = own * fb[b]
        for a in range(total):
            mixed = mixed + (2.0 * penalty / trace_value) * (
                gram[a : a + 1, b : b + 1] * fb[a]
                - gram[a : a + 1, LANES // 2 + b : LANES // 2 + b + 1] * sw[a])
        out_velocity[b] = momentum * velocity[b] + mixed

    a_copies = []
    for r in range(rank):
        across(r, z).wait_recv()
        y[r, rows_for(z, core), :] += xbuf[z, r]

        @pl.when(z > 0)
        def _():
            rightward(r, z).wait_recv()
            y[r, rows_for(z, core), :] += right_buf[z, r]

        @pl.when(z < zs - 1)
        def _():
            leftward(r, z).wait_recv()
            y[r, rows_for(z, core), :] += left_buf[z, r]

        for s in range(1, n_col):
            peer = col_peer(s)
            a_copies.append(copy(y.at[r, rows_of(i * n_col + peer, part)], ab.at[j * rank + r],
                                 a_send.at[s, r], a_recv.at[s, r], (i, peer)))
            a_copies[-1].start()
        ab[j * rank + r] = y[r, rows_of(i * n_col + j, part), :]

    for t in range(zs):
        for r in range(rank):
            across(r, lax.rem(z + t + 1, zs)).wait_send()
    for t in range(zs - 1):
        for r in range(rank):
            @pl.when(t >= z)
            def _():
                rightward(r, z + zs - 1 - t).wait_send()

            @pl.when(t >= zs - 1 - z)
            def _():
                leftward(r, t - (zs - 1 - z)).wait_send()

    for c in a_copies:
        c.wait()
    new_velocity = out_velocity[...] - rate * ab[...]
    out_velocity[...] = new_velocity
    out_factor[...] = fb[...] - step_size * new_velocity


def interleave(x):
    n, two, m = x.shape
    return x.reshape(n, two, m // LANES, LANES).transpose(0, 2, 1, 3).reshape(n, two * m // LANES, LANES)


def separate(x):
    n, rows, lanes = x.shape
    return x.reshape(n, rows // 2, 2, lanes).transpose(0, 2, 1, 3).reshape(n, 2, rows // 2 * lanes)


def shards(n_set, n_col, factor, velocity, labels, counts):
    rank, _, order = factor.shape
    total = rank * n_col
    left, rsize = 2**QA, 2**QB
    chunk = left // n_col
    wide = 2 * order // LANES
    block = wide // n_set
    part = block // n_col
    zs = n_set // 2
    f32, bf16 = jnp.float32, jnp.bfloat16
    vmem = pl.BlockSpec(memory_space=pltpu.VMEM)
    dma = pltpu.SemaphoreType.DMA
    out = jax.ShapeDtypeStruct((total, part, LANES), f32)
    new_factor, new_velocity = pl.pallas_call(
        functools.partial(kernel, n_set, n_col),
        out_shape=(out, out),
        in_specs=[pl.BlockSpec(memory_space=pltpu.SMEM), vmem, vmem, vmem],
        out_specs=(vmem, vmem),
        scratch_shapes=[
            pltpu.VMEM((rsize, rsize), bf16),
            pltpu.VMEM((2 * rank, left, rsize), bf16),
            pltpu.VMEM((2 * rank, left, rsize), bf16),
            pltpu.VMEM((2 * rank, left, rsize), f32),
            pltpu.VMEM((rank, wide, LANES), f32),
            pltpu.VMEM((n_col, chunk + 8, rsize), f32),
            pltpu.VMEM((n_col, chunk + 8, rsize), f32),
            pltpu.VMEM((chunk, rsize), f32),
            pltpu.VMEM((n_col, chunk, rsize), f32),
            pltpu.VMEM((total, part, LANES), f32),
            pltpu.VMEM((total, part, LANES), f32),
            pltpu.VMEM((total, part, LANES), f32),
            pltpu.VMEM((8 + total, LANES), f32),
            pltpu.VMEM((n_col, 8 + total, LANES), f32),
            pltpu.VMEM((8 + total, LANES), f32),
            pltpu.VMEM((n_set, 8 + total, LANES), f32),
            pltpu.VMEM((zs, rank, block, LANES), f32),
            pltpu.VMEM((zs, rank, block, LANES), f32),
            pltpu.VMEM((zs, rank, block, LANES), f32),
            dma((n_col,)), dma((n_col,)), dma((n_col,)), dma((n_col,)), dma((n_col,)), dma((n_col,)),
            dma((n_col,)), dma((n_col,)), dma((n_set,)), dma((n_set,)),
            dma((zs, rank)), dma((zs, rank)), dma((zs, rank)), dma((zs, rank)), dma((zs, rank)), dma((zs, rank)),
            dma((n_col, rank)), dma((n_col, rank)),
        ],
        compiler_params=pltpu.CompilerParams(
            collective_id=0, has_side_effects=True, vmem_limit_bytes=48 * 2**20),
        name="tomography_step",
    )(labels, interleave(factor), interleave(velocity), counts.reshape(order // LANES, LANES))
    return separate(new_factor), separate(new_velocity)


def solution(mesh):
    in_specs = (P("col", None, None), P(None, None, ("set", "col")), P("set", None), P("set", None))
    out_specs = (P(None, None, ("set", "col")), P(None, None, ("set", "col")))
    body = functools.partial(shards, mesh.shape["set"], mesh.shape["col"])
    return jax.shard_map(body, mesh=mesh, in_specs=in_specs, out_specs=out_specs, check_vma=False)
```

```python
import functools

import jax
import jax.numpy as jnp
from jax import lax
from jax.experimental import pallas as pl
from jax.experimental.pallas import tpu as pltpu
from jax.sharding import PartitionSpec as P

QA = 8
QB = 9
LANES = 128

mixing = 0.1
penalty = 8.0
momentum = 0.9
step_size = 0.5
count_norm = 8.0
MESH = pl.DeviceIdType.MESH


def fold_parity(x):
    x = x ^ (x >> 8)
    x = x ^ (x >> 4)
    x = x ^ (x >> 2)
    x = x ^ (x >> 1)
    return x & 1


def bit_count(x):
    x = x - ((x >> 1) & 0x55555)
    x = (x & 0x33333) + ((x >> 2) & 0x33333)
    x = (x + (x >> 4)) & 0xF0F0F
    return (x + (x >> 8) + (x >> 16)) & 0xFF


def sign_matrix(mask, size):
    row = lax.broadcasted_iota(jnp.int32, (size, size), 0)
    col = lax.broadcasted_iota(jnp.int32, (size, size), 1)
    sign = 1 - 2 * fold_parity(row & col & mask)
    keep = ((row ^ col) & (mask ^ (size - 1))) == 0
    return jnp.where(keep, sign, 0).astype(jnp.float32).astype(jnp.bfloat16)


def split(x):
    high = x.astype(jnp.bfloat16)
    return high, (x - high.astype(jnp.float32)).astype(jnp.bfloat16)


def dot(a, b):
    return jnp.dot(a, b, preferred_element_type=jnp.float32)


def kernel(n_set, n_col, labels, factor_hbm, velocity_hbm, counts_hbm, out_factor, out_base, out_adjoint,
           factor, velocity, counts, hb, high, low, g, y, psend, precv, wown, wrecv, fb, sw, ab, stat, stat_col, stat_sum, stat_all,
           xbuf, right_buf, left_buf,
           f_send, f_recv, p_send, p_recv, w_send, w_recv, c_send, c_recv, s_send, s_recv,
           x_send, x_recv, r_send, r_recv, l_send, l_recv, a_send, a_recv, load_sem):
    rank = factor.shape[0]
    left, rsize = 2**QA, 2**QB
    order = left * rsize
    tiles = rsize // LANES
    total = n_col * rank
    chunk = left // n_col
    block = factor.shape[1] // n_set
    part = block // n_col
    zs = n_set // 2
    i = lax.axis_index("set")
    j = lax.axis_index("col")
    z, core = i // 2, i % 2

    def col_peer(s):
        return lax.rem(j + s, n_col)

    def set_peer(s):
        return lax.rem(i + s, n_set)

    def rows_of(index, size):
        return pl.ds(pl.multiple_of(index * size, size), size)

    loads = [pltpu.make_async_copy(factor_hbm.at[r], factor.at[r], load_sem.at[r]) for r in range(rank)]
    loads.append(pltpu.make_async_copy(counts_hbm, counts, load_sem.at[rank]))
    loads.append(pltpu.make_async_copy(velocity_hbm, velocity, load_sem.at[rank + 1]))
    for load in loads:
        load.start()
    barrier = pltpu.get_barrier_semaphore()
    for s in range(1, n_col):
        pl.semaphore_signal(barrier, inc=1, device_id=(i, col_peer(s)), device_id_type=MESH)
    for s in range(1, n_set):
        pl.semaphore_signal(barrier, inc=1, device_id=(set_peer(s), j), device_id_type=MESH)

    def copy(src, dst, send, recv, where):
        return pltpu.make_async_remote_copy(
            src_ref=src, dst_ref=dst, send_sem=send, recv_sem=recv, device_id=where, device_id_type=MESH)

    nonz = jnp.int32(0)
    ymask = jnp.int32(0)
    scale = jnp.float32(1.0)
    for q in range(QA + QB):
        label = labels[0, q]
        bit = 1 << (QA + QB - 1 - q)
        nonz = nonz + jnp.where(label == 2, 0, bit)
        ymask = ymask + jnp.where(label == 1, bit, 0)
        scale = scale * jnp.where(label == 2, 1.0, 0.5).astype(jnp.float32)
    ha = sign_matrix(nonz >> QB, left)
    hb[...] = sign_matrix(nonz & (rsize - 1), rsize)

    index = (lax.broadcasted_iota(jnp.int32, (left, LANES), 0) * rsize
             + lax.broadcasted_iota(jnp.int32, (left, LANES), 1))

    def phases(b):
        phase = bit_count((index + b * LANES) & ymask) & 3
        odd = (phase & 1) == 1
        late = (1 - 2 * (phase >> 1)).astype(jnp.float32)
        mid = (1 - 2 * ((phase ^ (phase >> 1)) & 1)).astype(jnp.float32)
        return odd, late, mid

    for load in loads[:rank]:
        load.wait()
    square = jnp.zeros((left, LANES), jnp.float32)
    for b in range(tiles):
        odd, late, mid = phases(b)
        lanes = slice(b * LANES, (b + 1) * LANES)
        for r in range(rank):
            re = factor[r, pl.ds(2 * b, left, stride=2 * tiles), :]
            im = factor[r, pl.ds(2 * b + 1, left, stride=2 * tiles), :]
            square = square + re * re + im * im
            for c, x in enumerate((jnp.where(odd, im, re) * late, jnp.where(odd, re, im) * mid)):
                xh, xl = split(x)
                high[2 * r + c, :, lanes] = xh
                low[2 * r + c, :, lanes] = xl
    for rc in range(2 * rank):
        first = dot(ha, high[rc]) + dot(ha, low[rc])
        xh, xl = split(first)
        high[rc] = xh
        low[rc] = xl
    pl.semaphore_wait(barrier, n_col - 1 + n_set - 1)
    trace_part = jnp.sum(jnp.sum(square, axis=0, keepdims=True), axis=1, keepdims=True)

    p_copies = []
    for s in list(range(1, n_col)) + [0]:
        peer = col_peer(s)
        rows = rows_of(peer, chunk)
        xh = high[:, rows, :].reshape(2 * rank * chunk, rsize)
        xl = low[:, rows, :].reshape(2 * rank * chunk, rsize)
        second = (dot(xh, hb[...]) + dot(xl, hb[...])).reshape(2 * rank, chunk, rsize)
        g[:, rows, :] = second
        psend[s, :chunk, :] = scale * jnp.sum(second * second, axis=0)
        psend[s, chunk:, :] = jnp.broadcast_to(trace_part, (8, rsize))
        if s:
            p_copies.append(copy(psend.at[s], precv.at[s], p_send.at[s], p_recv.at[s], (i, peer)))
            p_copies[-1].start()

    prob = psend[0]
    for s, c in enumerate(p_copies, 1):
        c.wait()
        prob = prob + precv[s]
    trace_value = prob[chunk : chunk + 1, :1]
    prob = prob[:chunk]
    quasi = (1.0 - mixing) * prob / trace_value + mixing / order
    loads[rank].wait()
    count = jnp.concatenate(
        [counts[pl.ds(j * (chunk * tiles) + b, chunk, stride=tiles), :] for b in range(tiles)], axis=1
    ).astype(jnp.float32)
    weight = count / (count_norm * order * quasi)
    wown[...] = weight
    w_copies = []
    for s in range(1, n_col):
        w_copies.append(copy(wown, wrecv.at[s], w_send.at[s], w_recv.at[s], (i, col_peer(s))))
        w_copies[-1].start()
    ratio = jnp.sum((weight * prob / trace_value).reshape(chunk // 8, 8, rsize), axis=0)
    folded = ratio[:, :LANES]
    for b in range(1, tiles):
        folded = folded + ratio[:, b * LANES : (b + 1) * LANES]
    stat[:8, :] = folded

    mine = pl.ds(j * rank, rank)
    f_copies = []
    for s in range(1, n_col):
        peer = col_peer(s)
        f_copies.append(copy(factor.at[:, rows_of(i * n_col + peer, part)], fb.at[mine],
                             f_send.at[s], f_recv.at[s], (i, peer)))
        f_copies[-1].start()

    for s in range(n_col):
        if s:
            w_copies[s - 1].wait()
            weight = wrecv[s]
        else:
            weight = wown[...]
        rows = rows_of(lax.rem(j - s + n_col, n_col), chunk)
        xh, xl = split((g[:, rows, :] * (weight * scale)[None]).reshape(2 * rank * chunk, rsize))
        xh, xl = split(dot(xh, hb[...]) + dot(xl, hb[...]))
        high[:, rows, :] = xh.reshape(2 * rank, chunk, rsize)
        low[:, rows, :] = xl.reshape(2 * rank, chunk, rsize)

    def rows_for(d, side):
        return rows_of(2 * d + side, block)

    def across(r, d):
        return copy(y.at[r, rows_for(d, 1 - core)], xbuf.at[d, r], x_send.at[d, r], x_recv.at[d, r],
                    (2 * z + 1 - core, j))

    def rightward(r, d):
        return copy(y.at[r, rows_for(d, core)], right_buf.at[d, r], r_send.at[d, r], r_recv.at[d, r],
                    (lax.rem(i + 2, n_set), j))

    def leftward(r, d):
        return copy(y.at[r, rows_for(d, core)], left_buf.at[d, r], l_send.at[d, r], l_recv.at[d, r],
                    (lax.rem(i + n_set - 2, n_set), j))

    odd_late_mid = [phases(b) for b in range(tiles)]
    for r in range(rank):
        re_all = dot(ha, high[2 * r]) + dot(ha, low[2 * r])
        im_all = dot(ha, high[2 * r + 1]) + dot(ha, low[2 * r + 1])
        for b in range(tiles):
            odd, late, mid = odd_late_mid[b]
            re = re_all[:, b * LANES : (b + 1) * LANES]
            im = im_all[:, b * LANES : (b + 1) * LANES]
            y[r, pl.ds(2 * b, left, stride=2 * tiles), :] = jnp.where(odd, im, re) * mid
            y[r, pl.ds(2 * b + 1, left, stride=2 * tiles), :] = jnp.where(odd, re, im) * late
        for t in range(zs - 1):
            @pl.when(t >= z)
            def _():
                across(r, z + zs - 1 - t).start()

            @pl.when(t >= zs - 1 - z)
            def _():
                across(r, t - (zs - 1 - z)).start()
        across(r, z).start()

    for t in range(zs - 1):
        for r in range(rank):
            @pl.when(t >= z)
            def _():
                d = z + zs - 1 - t
                across(r, d).wait_recv()
                y[r, rows_for(d, core), :] += xbuf[d, r]

                @pl.when(z > 0)
                def _():
                    rightward(r, d).wait_recv()
                    y[r, rows_for(d, core), :] += right_buf[d, r]

                rightward(r, d).start()

            @pl.when(t >= zs - 1 - z)
            def _():
                d = t - (zs - 1 - z)
                across(r, d).wait_recv()
                y[r, rows_for(d, core), :] += xbuf[d, r]

                @pl.when(z < zs - 1)
                def _():
                    leftward(r, d).wait_recv()
                    y[r, rows_for(d, core), :] += left_buf[d, r]

                leftward(r, d).start()

        if t == 0:
            for r in range(rank):
                fb[j * rank + r] = factor[r, rows_of(i * n_col + j, part), :]
            for c in f_copies:
                c.wait()
            every = fb[...].reshape(total * part, LANES)
            parity = lax.broadcasted_iota(jnp.int32, every.shape, 0) & 1
            swapped = jnp.where(parity == 0, pltpu.roll(every, total * part - 1, 0), -pltpu.roll(every, 1, 0))
            sw[...] = swapped.reshape(total, part, LANES)
            lane = lax.broadcasted_iota(jnp.int32, (total, LANES), 1)
            gram = jnp.zeros((total, LANES), jnp.float32)
            for b in range(total):
                real = jnp.sum(jnp.sum(fb[...] * fb[b][None], axis=1), axis=1, keepdims=True)
                imag = jnp.sum(jnp.sum(fb[...] * sw[b][None], axis=1), axis=1, keepdims=True)
                gram = jnp.where(lane == b, real, gram)
                gram = jnp.where(lane == LANES // 2 + b, imag, gram)
            stat[8:, :] = gram
            c_copies = []
            for s in range(1, n_col):
                c_copies.append(copy(stat, stat_col.at[s], c_send.at[s], c_recv.at[s], (i, col_peer(s))))
                c_copies[-1].start()
        if t == min(1, zs - 2):
            summed = stat[...]
            for s, c in enumerate(c_copies, 1):
                c.wait()
                summed = summed + stat_col[s]
            stat_sum[...] = summed
            s_copies = []
            for s in range(1, n_set):
                s_copies.append(copy(stat_sum, stat_all.at[s], s_send.at[s], s_recv.at[s], (set_peer(s), j)))
                s_copies[-1].start()

    summed = stat_sum[...]
    for s, c in enumerate(s_copies, 1):
        c.wait()
        summed = summed + stat_all[s]
    ratio_total = jnp.sum(jnp.sum(summed[:8], axis=0, keepdims=True), axis=1, keepdims=True)
    gram = summed[8:]
    purity = jnp.sum(jnp.sum(gram * gram, axis=0, keepdims=True), axis=1, keepdims=True) / (trace_value * trace_value)
    settings_all = n_set * labels.shape[0]
    rate = (1.0 - mixing) / settings_all
    own = rate * ratio_total - 2.0 * penalty * purity
    loads[rank + 1].wait()
    for b in range(total):
        mixed = own * fb[b]
        for a in range(total):
            mixed = mixed + (2.0 * penalty / trace_value) * (
                gram[a : a + 1, b : b + 1] * fb[a]
                - gram[a : a + 1, LANES // 2 + b : LANES // 2 + b + 1] * sw[a])
        out_base[b] = momentum * velocity[b] + mixed
    out_factor[...] = fb[...]

    a_copies = []
    for r in range(rank):
        across(r, z).wait_recv()
        y[r, rows_for(z, core), :] += xbuf[z, r]

        @pl.when(z > 0)
        def _():
            rightward(r, z).wait_recv()
            y[r, rows_for(z, core), :] += right_buf[z, r]

        @pl.when(z < zs - 1)
        def _():
            leftward(r, z).wait_recv()
            y[r, rows_for(z, core), :] += left_buf[z, r]

        for s in range(1, n_col):
            peer = col_peer(s)
            a_copies.append(copy(y.at[r, rows_of(i * n_col + peer, part)], ab.at[j * rank + r],
                                 a_send.at[s, r], a_recv.at[s, r], (i, peer)))
            a_copies[-1].start()
        ab[j * rank + r] = y[r, rows_of(i * n_col + j, part), :]

    for t in range(zs):
        for r in range(rank):
            across(r, lax.rem(z + t + 1, zs)).wait_send()
    for t in range(zs - 1):
        for r in range(rank):
            @pl.when(t >= z)
            def _():
                rightward(r, z + zs - 1 - t).wait_send()

            @pl.when(t >= zs - 1 - z)
            def _():
                leftward(r, t - (zs - 1 - z)).wait_send()

    for c in a_copies:
        c.wait()
    out_adjoint[...] = rate * ab[...]


def interleave(x):
    n, two, m = x.shape
    return x.reshape(n, two, m // LANES, LANES).transpose(0, 2, 1, 3).reshape(n, two * m // LANES, LANES)


def separate(x):
    n, rows, lanes = x.shape
    return x.reshape(n, rows // 2, 2, lanes).transpose(0, 2, 1, 3).reshape(n, 2, rows // 2 * lanes)


def shards(n_set, n_col, factor, velocity, labels, counts):
    rank, _, order = factor.shape
    total = rank * n_col
    left, rsize = 2**QA, 2**QB
    chunk = left // n_col
    wide = 2 * order // LANES
    block = wide // n_set
    part = block // n_col
    zs = n_set // 2
    f32, bf16 = jnp.float32, jnp.bfloat16
    vmem = pl.BlockSpec(memory_space=pltpu.VMEM)
    hbm = pl.BlockSpec(memory_space=pltpu.HBM)
    dma = pltpu.SemaphoreType.DMA
    out = jax.ShapeDtypeStruct((total, part, LANES), f32)
    kept, base, adjoint = pl.pallas_call(
        functools.partial(kernel, n_set, n_col),
        out_shape=(out, out, out),
        in_specs=[pl.BlockSpec(memory_space=pltpu.SMEM), hbm, hbm, hbm],
        out_specs=(vmem, vmem, vmem),
        scratch_shapes=[
            pltpu.VMEM((rank, wide, LANES), f32),
            pltpu.VMEM((total, part, LANES), f32),
            pltpu.VMEM((order // LANES, LANES), jnp.int32),
            pltpu.VMEM((rsize, rsize), bf16),
            pltpu.VMEM((2 * rank, left, rsize), bf16),
            pltpu.VMEM((2 * rank, left, rsize), bf16),
            pltpu.VMEM((2 * rank, left, rsize), f32),
            pltpu.VMEM((rank, wide, LANES), f32),
            pltpu.VMEM((n_col, chunk + 8, rsize), f32),
            pltpu.VMEM((n_col, chunk + 8, rsize), f32),
            pltpu.VMEM((chunk, rsize), f32),
            pltpu.VMEM((n_col, chunk, rsize), f32),
            pltpu.VMEM((total, part, LANES), f32),
            pltpu.VMEM((total, part, LANES), f32),
            pltpu.VMEM((total, part, LANES), f32),
            pltpu.VMEM((8 + total, LANES), f32),
            pltpu.VMEM((n_col, 8 + total, LANES), f32),
            pltpu.VMEM((8 + total, LANES), f32),
            pltpu.VMEM((n_set, 8 + total, LANES), f32),
            pltpu.VMEM((zs, rank, block, LANES), f32),
            pltpu.VMEM((zs, rank, block, LANES), f32),
            pltpu.VMEM((zs, rank, block, LANES), f32),
            dma((n_col,)), dma((n_col,)), dma((n_col,)), dma((n_col,)), dma((n_col,)), dma((n_col,)),
            dma((n_col,)), dma((n_col,)), dma((n_set,)), dma((n_set,)),
            dma((zs, rank)), dma((zs, rank)), dma((zs, rank)), dma((zs, rank)), dma((zs, rank)), dma((zs, rank)),
            dma((n_col, rank)), dma((n_col, rank)), dma((rank + 2,)),
        ],
        compiler_params=pltpu.CompilerParams(
            collective_id=0, has_side_effects=True, vmem_limit_bytes=60 * 2**20),
        name="tomography_step",
    )(labels, interleave(factor), interleave(velocity), counts.reshape(order // LANES, LANES))
    new_velocity = separate(base) - separate(adjoint)
    return separate(kept) - step_size * new_velocity, new_velocity


def solution(mesh):
    in_specs = (P("col", None, None), P(None, None, ("set", "col")), P("set", None), P("set", None))
    out_specs = (P(None, None, ("set", "col")), P(None, None, ("set", "col")))
    body = functools.partial(shards, mesh.shape["set"], mesh.shape["col"])
    return jax.shard_map(body, mesh=mesh, in_specs=in_specs, out_specs=out_specs, check_vma=False)
```

```python
import functools

import jax
import jax.numpy as jnp
from jax import lax
from jax.experimental import pallas as pl
from jax.experimental.pallas import tpu as pltpu
from jax.sharding import PartitionSpec as P

QA = 8
QB = 9
LANES = 128

mixing = 0.1
penalty = 8.0
momentum = 0.9
step_size = 0.5
count_norm = 8.0
MESH = pl.DeviceIdType.MESH


def fold_parity(x):
    x = x ^ (x >> 8)
    x = x ^ (x >> 4)
    x = x ^ (x >> 2)
    x = x ^ (x >> 1)
    return x & 1


def bit_count(x):
    x = x - ((x >> 1) & 0x55555)
    x = (x & 0x33333) + ((x >> 2) & 0x33333)
    x = (x + (x >> 4)) & 0xF0F0F
    return (x + (x >> 8) + (x >> 16)) & 0xFF


def sign_matrix(mask, size):
    row = lax.broadcasted_iota(jnp.int32, (size, size), 0)
    col = lax.broadcasted_iota(jnp.int32, (size, size), 1)
    sign = 1 - 2 * fold_parity(row & col & mask)
    keep = ((row ^ col) & (mask ^ (size - 1))) == 0
    return jnp.where(keep, sign, 0).astype(jnp.float32).astype(jnp.bfloat16)


def split(x):
    high = x.astype(jnp.bfloat16)
    return high, (x - high.astype(jnp.float32)).astype(jnp.bfloat16)


def dot(a, b):
    return jnp.dot(a, b, preferred_element_type=jnp.float32)


def kernel(n_set, n_col, labels, factor_hbm, velocity_hbm, counts_hbm, out_factor, out_velocity,
           factor, velocity, counts, hb, high, low, g, y, psend, precv, wown, wrecv, fb, sw, ab, stat, stat_col, stat_sum, stat_all,
           xbuf, right_buf, left_buf,
           f_send, f_recv, p_send, p_recv, w_send, w_recv, c_send, c_recv, s_send, s_recv,
           x_send, x_recv, r_send, r_recv, l_send, l_recv, a_send, a_recv, load_sem):
    rank = factor.shape[0]
    left, rsize = 2**QA, 2**QB
    order = left * rsize
    tiles = rsize // LANES
    total = n_col * rank
    chunk = left // n_col
    block = factor.shape[1] // n_set
    part = block // n_col
    zs = n_set // 2
    i = lax.axis_index("set")
    j = lax.axis_index("col")
    z, core = i // 2, i % 2

    def col_peer(s):
        return lax.rem(j + s, n_col)

    def set_peer(s):
        return lax.rem(i + s, n_set)

    def rows_of(index, size):
        return pl.ds(pl.multiple_of(index * size, size), size)

    loads = [pltpu.make_async_copy(factor_hbm.at[r], factor.at[r], load_sem.at[r]) for r in range(rank)]
    loads.append(pltpu.make_async_copy(counts_hbm, counts, load_sem.at[rank]))
    loads.append(pltpu.make_async_copy(velocity_hbm, velocity, load_sem.at[rank + 1]))
    for load in loads:
        load.start()
    barrier = pltpu.get_barrier_semaphore()
    for s in range(1, n_col):
        pl.semaphore_signal(barrier, inc=1, device_id=(i, col_peer(s)), device_id_type=MESH)
    for s in range(1, n_set):
        pl.semaphore_signal(barrier, inc=1, device_id=(set_peer(s), j), device_id_type=MESH)

    def copy(src, dst, send, recv, where):
        return pltpu.make_async_remote_copy(
            src_ref=src, dst_ref=dst, send_sem=send, recv_sem=recv, device_id=where, device_id_type=MESH)

    nonz = jnp.int32(0)
    ymask = jnp.int32(0)
    scale = jnp.float32(1.0)
    for q in range(QA + QB):
        label = labels[0, q]
        bit = 1 << (QA + QB - 1 - q)
        nonz = nonz + jnp.where(label == 2, 0, bit)
        ymask = ymask + jnp.where(label == 1, bit, 0)
        scale = scale * jnp.where(label == 2, 1.0, 0.5).astype(jnp.float32)
    ha = sign_matrix(nonz >> QB, left)
    hb[...] = sign_matrix(nonz & (rsize - 1), rsize)

    index = (lax.broadcasted_iota(jnp.int32, (left, LANES), 0) * rsize
             + lax.broadcasted_iota(jnp.int32, (left, LANES), 1))

    def phases(b):
        phase = bit_count((index + b * LANES) & ymask) & 3
        odd = (phase & 1) == 1
        late = (1 - 2 * (phase >> 1)).astype(jnp.float32)
        mid = (1 - 2 * ((phase ^ (phase >> 1)) & 1)).astype(jnp.float32)
        return odd, late, mid

    for load in loads[:rank]:
        load.wait()
    square = jnp.zeros((left, LANES), jnp.float32)
    for b in range(tiles):
        odd, late, mid = phases(b)
        lanes = slice(b * LANES, (b + 1) * LANES)
        for r in range(rank):
            re = factor[r, pl.ds(2 * b, left, stride=2 * tiles), :]
            im = factor[r, pl.ds(2 * b + 1, left, stride=2 * tiles), :]
            square = square + re * re + im * im
            for c, x in enumerate((jnp.where(odd, im, re) * late, jnp.where(odd, re, im) * mid)):
                xh, xl = split(x)
                high[2 * r + c, :, lanes] = xh
                low[2 * r + c, :, lanes] = xl
    for rc in range(2 * rank):
        first = dot(ha, high[rc]) + dot(ha, low[rc])
        xh, xl = split(first)
        high[rc] = xh
        low[rc] = xl
    pl.semaphore_wait(barrier, n_col - 1 + n_set - 1)
    trace_part = jnp.sum(jnp.sum(square, axis=0, keepdims=True), axis=1, keepdims=True)

    p_copies = []
    for s in list(range(1, n_col)) + [0]:
        peer = col_peer(s)
        rows = rows_of(peer, chunk)
        xh = high[:, rows, :].reshape(2 * rank * chunk, rsize)
        xl = low[:, rows, :].reshape(2 * rank * chunk, rsize)
        second = (dot(xh, hb[...]) + dot(xl, hb[...])).reshape(2 * rank, chunk, rsize)
        g[:, rows, :] = second
        psend[s, :chunk, :] = scale * jnp.sum(second * second, axis=0)
        psend[s, chunk:, :] = jnp.broadcast_to(trace_part, (8, rsize))
        if s:
            p_copies.append(copy(psend.at[s], precv.at[s], p_send.at[s], p_recv.at[s], (i, peer)))
            p_copies[-1].start()

    prob = psend[0]
    for s, c in enumerate(p_copies, 1):
        c.wait()
        prob = prob + precv[s]
    trace_value = prob[chunk : chunk + 1, :1]
    prob = prob[:chunk]
    quasi = (1.0 - mixing) * prob / trace_value + mixing / order
    loads[rank].wait()
    count = jnp.concatenate(
        [counts[pl.ds(j * (chunk * tiles) + b, chunk, stride=tiles), :] for b in range(tiles)], axis=1
    ).astype(jnp.float32)
    weight = count / (count_norm * order * quasi)
    wown[...] = weight
    w_copies = []
    for s in range(1, n_col):
        w_copies.append(copy(wown, wrecv.at[s], w_send.at[s], w_recv.at[s], (i, col_peer(s))))
        w_copies[-1].start()
    ratio = jnp.sum((weight * prob / trace_value).reshape(chunk // 8, 8, rsize), axis=0)
    folded = ratio[:, :LANES]
    for b in range(1, tiles):
        folded = folded + ratio[:, b * LANES : (b + 1) * LANES]
    stat[:8, :] = folded

    for s in range(n_col):
        if s:
            w_copies[s - 1].wait()
            weight = wrecv[s]
        else:
            weight = wown[...]
        rows = rows_of(lax.rem(j - s + n_col, n_col), chunk)
        xh, xl = split((g[:, rows, :] * (weight * scale)[None]).reshape(2 * rank * chunk, rsize))
        xh, xl = split(dot(xh, hb[...]) + dot(xl, hb[...]))
        high[:, rows, :] = xh.reshape(2 * rank, chunk, rsize)
        low[:, rows, :] = xl.reshape(2 * rank, chunk, rsize)

    mine = pl.ds(j * rank, rank)
    f_copies = []
    for s in range(1, n_col):
        peer = col_peer(s)
        f_copies.append(copy(factor.at[:, rows_of(i * n_col + peer, part)], fb.at[mine],
                             f_send.at[s], f_recv.at[s], (i, peer)))
        f_copies[-1].start()

    def rows_for(d, side):
        return rows_of(2 * d + side, block)

    def across(r, d):
        return copy(y.at[r, rows_for(d, 1 - core)], xbuf.at[d, r], x_send.at[d, r], x_recv.at[d, r],
                    (2 * z + 1 - core, j))

    def rightward(r, d):
        return copy(y.at[r, rows_for(d, core)], right_buf.at[d, r], r_send.at[d, r], r_recv.at[d, r],
                    (lax.rem(i + 2, n_set), j))

    def leftward(r, d):
        return copy(y.at[r, rows_for(d, core)], left_buf.at[d, r], l_send.at[d, r], l_recv.at[d, r],
                    (lax.rem(i + n_set - 2, n_set), j))

    odd_late_mid = [phases(b) for b in range(tiles)]
    for r in range(rank):
        re_all = dot(ha, high[2 * r]) + dot(ha, low[2 * r])
        im_all = dot(ha, high[2 * r + 1]) + dot(ha, low[2 * r + 1])
        for b in range(tiles):
            odd, late, mid = odd_late_mid[b]
            re = re_all[:, b * LANES : (b + 1) * LANES]
            im = im_all[:, b * LANES : (b + 1) * LANES]
            y[r, pl.ds(2 * b, left, stride=2 * tiles), :] = jnp.where(odd, im, re) * mid
            y[r, pl.ds(2 * b + 1, left, stride=2 * tiles), :] = jnp.where(odd, re, im) * late
        for t in range(zs - 1):
            @pl.when(t >= z)
            def _():
                across(r, z + zs - 1 - t).start()

            @pl.when(t >= zs - 1 - z)
            def _():
                across(r, t - (zs - 1 - z)).start()
        across(r, z).start()

    for t in range(zs - 1):
        for r in range(rank):
            @pl.when(t >= z)
            def _():
                d = z + zs - 1 - t
                across(r, d).wait_recv()
                y[r, rows_for(d, core), :] += xbuf[d, r]

                @pl.when(z > 0)
                def _():
                    rightward(r, d).wait_recv()
                    y[r, rows_for(d, core), :] += right_buf[d, r]

                @pl.when(t > z)
                def _():
                    rightward(r, d + 1).wait_send()

                rightward(r, d).start()

            @pl.when(t >= zs - 1 - z)
            def _():
                d = t - (zs - 1 - z)
                across(r, d).wait_recv()
                y[r, rows_for(d, core), :] += xbuf[d, r]

                @pl.when(z < zs - 1)
                def _():
                    leftward(r, d).wait_recv()
                    y[r, rows_for(d, core), :] += left_buf[d, r]

                @pl.when(t > zs - 1 - z)
                def _():
                    leftward(r, d - 1).wait_send()

                leftward(r, d).start()

        if t == 0:
            for r in range(rank):
                fb[j * rank + r] = factor[r, rows_of(i * n_col + j, part), :]
            for c in f_copies:
                c.wait()
            every = fb[...].reshape(total * part, LANES)
            parity = lax.broadcasted_iota(jnp.int32, every.shape, 0) & 1
            swapped = jnp.where(parity == 0, pltpu.roll(every, total * part - 1, 0), -pltpu.roll(every, 1, 0))
            sw[...] = swapped.reshape(total, part, LANES)
            lane = lax.broadcasted_iota(jnp.int32, (total, LANES), 1)
            gram = jnp.zeros((total, LANES), jnp.float32)
            for b in range(total):
                real = jnp.sum(jnp.sum(fb[...] * fb[b][None], axis=1), axis=1, keepdims=True)
                imag = jnp.sum(jnp.sum(fb[...] * sw[b][None], axis=1), axis=1, keepdims=True)
                gram = jnp.where(lane == b, real, gram)
                gram = jnp.where(lane == LANES // 2 + b, imag, gram)
            stat[8:, :] = gram
            c_copies = []
            for s in range(1, n_col):
                c_copies.append(copy(stat, stat_col.at[s], c_send.at[s], c_recv.at[s], (i, col_peer(s))))
                c_copies[-1].start()
        if t == min(1, zs - 2):
            summed = stat[...]
            for s, c in enumerate(c_copies, 1):
                c.wait()
                summed = summed + stat_col[s]
            stat_sum[...] = summed
            s_copies = []
            for s in range(1, n_set):
                s_copies.append(copy(stat_sum, stat_all.at[s], s_send.at[s], s_recv.at[s], (set_peer(s), j)))
                s_copies[-1].start()

    summed = stat_sum[...]
    for s, c in enumerate(s_copies, 1):
        c.wait()
        summed = summed + stat_all[s]
    ratio_total = jnp.sum(jnp.sum(summed[:8], axis=0, keepdims=True), axis=1, keepdims=True)
    gram = summed[8:]
    purity = jnp.sum(jnp.sum(gram * gram, axis=0, keepdims=True), axis=1, keepdims=True) / (trace_value * trace_value)
    settings_all = n_set * labels.shape[0]
    rate = (1.0 - mixing) / settings_all
    own = rate * ratio_total - 2.0 * penalty * purity
    loads[rank + 1].wait()
    for b in range(total):
        mixed = own * fb[b]
        for a in range(total):
            mixed = mixed + (2.0 * penalty / trace_value) * (
                gram[a : a + 1, b : b + 1] * fb[a]
                - gram[a : a + 1, LANES // 2 + b : LANES // 2 + b + 1] * sw[a])
        out_velocity[b] = momentum * velocity[b] + mixed

    a_copies = []
    for r in range(rank):
        across(r, z).wait_recv()
        y[r, rows_for(z, core), :] += xbuf[z, r]

        @pl.when(z > 0)
        def _():
            rightward(r, z).wait_recv()
            y[r, rows_for(z, core), :] += right_buf[z, r]

        @pl.when(z < zs - 1)
        def _():
            leftward(r, z).wait_recv()
            y[r, rows_for(z, core), :] += left_buf[z, r]

        for s in range(1, n_col):
            peer = col_peer(s)
            a_copies.append(copy(y.at[r, rows_of(i * n_col + peer, part)], ab.at[j * rank + r],
                                 a_send.at[s, r], a_recv.at[s, r], (i, peer)))
            a_copies[-1].start()
        ab[j * rank + r] = y[r, rows_of(i * n_col + j, part), :]

    for t in range(zs):
        for r in range(rank):
            across(r, lax.rem(z + t + 1, zs)).wait_send()
    for r in range(rank):
        @pl.when(z < zs - 1)
        def _():
            rightward(r, z + 1).wait_send()

        @pl.when(z > 0)
        def _():
            leftward(r, z - 1).wait_send()

    for c in a_copies:
        c.wait()
    new_velocity = out_velocity[...] - rate * ab[...]
    out_velocity[...] = new_velocity
    out_factor[...] = fb[...] - step_size * new_velocity


def interleave(x):
    n, two, m = x.shape
    return x.reshape(n, two, m // LANES, LANES).transpose(0, 2, 1, 3).reshape(n, two * m // LANES, LANES)


def separate(x):
    n, rows, lanes = x.shape
    return x.reshape(n, rows // 2, 2, lanes).transpose(0, 2, 1, 3).reshape(n, 2, rows // 2 * lanes)


def shards(n_set, n_col, factor, velocity, labels, counts):
    rank, _, order = factor.shape
    total = rank * n_col
    left, rsize = 2**QA, 2**QB
    chunk = left // n_col
    wide = 2 * order // LANES
    block = wide // n_set
    part = block // n_col
    zs = n_set // 2
    f32, bf16 = jnp.float32, jnp.bfloat16
    vmem = pl.BlockSpec(memory_space=pltpu.VMEM)
    hbm = pl.BlockSpec(memory_space=pltpu.HBM)
    dma = pltpu.SemaphoreType.DMA
    out = jax.ShapeDtypeStruct((total, part, LANES), f32)
    new_factor, new_velocity = pl.pallas_call(
        functools.partial(kernel, n_set, n_col),
        out_shape=(out, out),
        in_specs=[pl.BlockSpec(memory_space=pltpu.SMEM), hbm, hbm, hbm],
        out_specs=(vmem, vmem),
        scratch_shapes=[
            pltpu.VMEM((rank, wide, LANES), f32),
            pltpu.VMEM((total, part, LANES), f32),
            pltpu.VMEM((order // LANES, LANES), jnp.int32),
            pltpu.VMEM((rsize, rsize), bf16),
            pltpu.VMEM((2 * rank, left, rsize), bf16),
            pltpu.VMEM((2 * rank, left, rsize), bf16),
            pltpu.VMEM((2 * rank, left, rsize), f32),
            pltpu.VMEM((rank, wide, LANES), f32),
            pltpu.VMEM((n_col, chunk + 8, rsize), f32),
            pltpu.VMEM((n_col, chunk + 8, rsize), f32),
            pltpu.VMEM((chunk, rsize), f32),
            pltpu.VMEM((n_col, chunk, rsize), f32),
            pltpu.VMEM((total, part, LANES), f32),
            pltpu.VMEM((total, part, LANES), f32),
            pltpu.VMEM((total, part, LANES), f32),
            pltpu.VMEM((8 + total, LANES), f32),
            pltpu.VMEM((n_col, 8 + total, LANES), f32),
            pltpu.VMEM((8 + total, LANES), f32),
            pltpu.VMEM((n_set, 8 + total, LANES), f32),
            pltpu.VMEM((zs, rank, block, LANES), f32),
            pltpu.VMEM((zs, rank, block, LANES), f32),
            pltpu.VMEM((zs, rank, block, LANES), f32),
            dma((n_col,)), dma((n_col,)), dma((n_col,)), dma((n_col,)), dma((n_col,)), dma((n_col,)),
            dma((n_col,)), dma((n_col,)), dma((n_set,)), dma((n_set,)),
            dma((zs, rank)), dma((zs, rank)), dma((zs, rank)), dma((zs, rank)), dma((zs, rank)), dma((zs, rank)),
            dma((n_col, rank)), dma((n_col, rank)), dma((rank + 2,)),
        ],
        compiler_params=pltpu.CompilerParams(
            collective_id=0, has_side_effects=True, vmem_limit_bytes=60 * 2**20),
        name="tomography_step",
    )(labels, interleave(factor), interleave(velocity), counts.reshape(order // LANES, LANES))
    return separate(new_factor), separate(new_velocity)


def solution(mesh):
    in_specs = (P("col", None, None), P(None, None, ("set", "col")), P("set", None), P("set", None))
    out_specs = (P(None, None, ("set", "col")), P(None, None, ("set", "col")))
    body = functools.partial(shards, mesh.shape["set"], mesh.shape["col"])
    return jax.shard_map(body, mesh=mesh, in_specs=in_specs, out_specs=out_specs, check_vma=False)
```

```python
import functools

import jax
import jax.numpy as jnp
from jax import lax
from jax.experimental import pallas as pl
from jax.experimental.pallas import tpu as pltpu
from jax.sharding import PartitionSpec as P

QA = 8
QB = 9
LANES = 128

mixing = 0.1
penalty = 8.0
momentum = 0.9
step_size = 0.5
count_norm = 8.0
MESH = pl.DeviceIdType.MESH


def fold_parity(x):
    x = x ^ (x >> 8)
    x = x ^ (x >> 4)
    x = x ^ (x >> 2)
    x = x ^ (x >> 1)
    return x & 1


def bit_count(x):
    x = x - ((x >> 1) & 0x55555)
    x = (x & 0x33333) + ((x >> 2) & 0x33333)
    x = (x + (x >> 4)) & 0xF0F0F
    return (x + (x >> 8) + (x >> 16)) & 0xFF


def sign_matrix(mask, size):
    row = lax.broadcasted_iota(jnp.int32, (size, size), 0)
    col = lax.broadcasted_iota(jnp.int32, (size, size), 1)
    sign = 1 - 2 * fold_parity(row & col & mask)
    keep = ((row ^ col) & (mask ^ (size - 1))) == 0
    return jnp.where(keep, sign, 0).astype(jnp.float32).astype(jnp.bfloat16)


def split(x):
    high = x.astype(jnp.bfloat16)
    return high, (x - high.astype(jnp.float32)).astype(jnp.bfloat16)


def dot(a, b):
    return jnp.dot(a, b, preferred_element_type=jnp.float32)


def kernel(n_set, n_col, labels, factor_hbm, velocity_hbm, counts_hbm, out_factor, out_velocity,
           factor, velocity, counts, hb, high, low, g, y, psend, precv, wown, wrecv, fb, sw, ab, stat, stat_col, stat_sum, stat_all,
           xbuf, right_buf, left_buf,
           f_send, f_recv, p_send, p_recv, w_send, w_recv, c_send, c_recv, s_send, s_recv,
           x_send, x_recv, r_send, r_recv, l_send, l_recv, a_send, a_recv, load_sem):
    rank = factor.shape[0]
    left, rsize = 2**QA, 2**QB
    order = left * rsize
    tiles = rsize // LANES
    total = n_col * rank
    chunk = left // n_col
    block = factor.shape[1] // n_set
    part = block // n_col
    zs = n_set // 2
    i = lax.axis_index("set")
    j = lax.axis_index("col")
    z, core = i // 2, i % 2

    def col_peer(s):
        return lax.rem(j + s, n_col)

    def set_peer(s):
        return lax.rem(i + s, n_set)

    def rows_of(index, size):
        return pl.ds(pl.multiple_of(index * size, size), size)

    loads = [pltpu.make_async_copy(factor_hbm.at[r], factor.at[r], load_sem.at[r]) for r in range(rank)]
    loads.append(pltpu.make_async_copy(counts_hbm, counts, load_sem.at[rank]))
    loads.append(pltpu.make_async_copy(velocity_hbm, velocity, load_sem.at[rank + 1]))
    for load in loads:
        load.start()
    barrier = pltpu.get_barrier_semaphore()
    for s in range(1, n_col):
        pl.semaphore_signal(barrier, inc=1, device_id=(i, col_peer(s)), device_id_type=MESH)
    for s in range(1, n_set):
        pl.semaphore_signal(barrier, inc=1, device_id=(set_peer(s), j), device_id_type=MESH)

    def copy(src, dst, send, recv, where):
        return pltpu.make_async_remote_copy(
            src_ref=src, dst_ref=dst, send_sem=send, recv_sem=recv, device_id=where, device_id_type=MESH)

    nonz = jnp.int32(0)
    ymask = jnp.int32(0)
    scale = jnp.float32(1.0)
    for q in range(QA + QB):
        label = labels[0, q]
        bit = 1 << (QA + QB - 1 - q)
        nonz = nonz + jnp.where(label == 2, 0, bit)
        ymask = ymask + jnp.where(label == 1, bit, 0)
        scale = scale * jnp.where(label == 2, 1.0, 0.5).astype(jnp.float32)
    ha = sign_matrix(nonz >> QB, left)
    hb[...] = sign_matrix(nonz & (rsize - 1), rsize)

    index = (lax.broadcasted_iota(jnp.int32, (left, LANES), 0) * rsize
             + lax.broadcasted_iota(jnp.int32, (left, LANES), 1))

    def phases(b):
        phase = bit_count((index + b * LANES) & ymask) & 3
        odd = (phase & 1) == 1
        late = (1 - 2 * (phase >> 1)).astype(jnp.float32)
        mid = (1 - 2 * ((phase ^ (phase >> 1)) & 1)).astype(jnp.float32)
        return odd, late, mid

    for load in loads[:rank]:
        load.wait()
    square = jnp.zeros((left, LANES), jnp.float32)
    for b in range(tiles):
        odd, late, mid = phases(b)
        lanes = slice(b * LANES, (b + 1) * LANES)
        for r in range(rank):
            re = factor[r, pl.ds(2 * b, left, stride=2 * tiles), :]
            im = factor[r, pl.ds(2 * b + 1, left, stride=2 * tiles), :]
            square = square + re * re + im * im
            for c, x in enumerate((jnp.where(odd, im, re) * late, jnp.where(odd, re, im) * mid)):
                xh, xl = split(x)
                high[2 * r + c, :, lanes] = xh
                low[2 * r + c, :, lanes] = xl
    for rc in range(2 * rank):
        first = dot(ha, high[rc]) + dot(ha, low[rc])
        xh, xl = split(first)
        high[rc] = xh
        low[rc] = xl
    pl.semaphore_wait(barrier, n_col - 1 + n_set - 1)
    trace_part = jnp.sum(jnp.sum(square, axis=0, keepdims=True), axis=1, keepdims=True)

    p_copies = []
    for s in list(range(1, n_col)) + [0]:
        peer = col_peer(s)
        rows = rows_of(peer, chunk)
        xh = high[:, rows, :].reshape(2 * rank * chunk, rsize)
        xl = low[:, rows, :].reshape(2 * rank * chunk, rsize)
        second = (dot(xh, hb[...]) + dot(xl, hb[...])).reshape(2 * rank, chunk, rsize)
        g[:, rows, :] = second
        psend[s, :chunk, :] = scale * jnp.sum(second * second, axis=0)
        psend[s, chunk:, :] = jnp.broadcast_to(trace_part, (8, rsize))
        if s:
            p_copies.append(copy(psend.at[s], precv.at[s], p_send.at[s], p_recv.at[s], (i, peer)))
            p_copies[-1].start()

    prob = psend[0]
    for s, c in enumerate(p_copies, 1):
        c.wait()
        prob = prob + precv[s]
    trace_value = prob[chunk : chunk + 1, :1]
    prob = prob[:chunk]
    quasi = (1.0 - mixing) * prob / trace_value + mixing / order
    loads[rank].wait()
    count = jnp.concatenate(
        [counts[pl.ds(j * (chunk * tiles) + b, chunk, stride=tiles), :] for b in range(tiles)], axis=1
    ).astype(jnp.float32)
    weight = count / (count_norm * order * quasi)
    wown[...] = weight
    w_copies = []
    for s in range(1, n_col):
        w_copies.append(copy(wown, wrecv.at[s], w_send.at[s], w_recv.at[s], (i, col_peer(s))))
        w_copies[-1].start()
    ratio = jnp.sum((weight * prob / trace_value).reshape(chunk // 8, 8, rsize), axis=0)
    folded = ratio[:, :LANES]
    for b in range(1, tiles):
        folded = folded + ratio[:, b * LANES : (b + 1) * LANES]
    stat[:8, :] = folded

    for s in range(n_col):
        if s:
            w_copies[s - 1].wait()
            weight = wrecv[s]
        else:
            weight = wown[...]
        rows = rows_of(lax.rem(j - s + n_col, n_col), chunk)
        xh, xl = split((g[:, rows, :] * (weight * scale)[None]).reshape(2 * rank * chunk, rsize))
        xh, xl = split(dot(xh, hb[...]) + dot(xl, hb[...]))
        high[:, rows, :] = xh.reshape(2 * rank, chunk, rsize)
        low[:, rows, :] = xl.reshape(2 * rank, chunk, rsize)

    mine = pl.ds(j * rank, rank)
    f_copies = []
    for s in range(1, n_col):
        peer = col_peer(s)
        f_copies.append(copy(factor.at[:, rows_of(i * n_col + peer, part)], fb.at[mine],
                             f_send.at[s], f_recv.at[s], (i, peer)))
        f_copies[-1].start()

    def rows_for(d, side):
        return rows_of(2 * d + side, block)

    def across(r, d):
        return copy(y.at[r, rows_for(d, 1 - core)], xbuf.at[d, r], x_send.at[d, r], x_recv.at[d, r],
                    (2 * z + 1 - core, j))

    def rightward(r, d):
        return copy(y.at[r, rows_for(d, core)], right_buf.at[d, r], r_send.at[d, r], r_recv.at[d, r],
                    (lax.rem(i + 2, n_set), j))

    def leftward(r, d):
        return copy(y.at[r, rows_for(d, core)], left_buf.at[d, r], l_send.at[d, r], l_recv.at[d, r],
                    (lax.rem(i + n_set - 2, n_set), j))

    odd_late_mid = [phases(b) for b in range(tiles)]
    for r in range(rank):
        re_all = dot(ha, high[2 * r]) + dot(ha, low[2 * r])
        im_all = dot(ha, high[2 * r + 1]) + dot(ha, low[2 * r + 1])
        for b in range(tiles):
            odd, late, mid = odd_late_mid[b]
            re = re_all[:, b * LANES : (b + 1) * LANES]
            im = im_all[:, b * LANES : (b + 1) * LANES]
            y[r, pl.ds(2 * b, left, stride=2 * tiles), :] = jnp.where(odd, im, re) * mid
            y[r, pl.ds(2 * b + 1, left, stride=2 * tiles), :] = jnp.where(odd, re, im) * late
        for t in range(zs - 1):
            @pl.when(t >= z)
            def _():
                across(r, z + zs - 1 - t).start()

            @pl.when(t >= zs - 1 - z)
            def _():
                across(r, t - (zs - 1 - z)).start()
        across(r, z).start()

    for t in range(zs - 1):
        for r in range(rank):
            @pl.when(t >= z)
            def _():
                d = z + zs - 1 - t
                across(r, d).wait_recv()
                y[r, rows_for(d, core), :] += xbuf[d, r]

                @pl.when(z > 0)
                def _():
                    rightward(r, d).wait_recv()
                    y[r, rows_for(d, core), :] += right_buf[d, r]

                @pl.when(t > z)
                def _():
                    rightward(r, d + 1).wait_send()

                rightward(r, d).start()

            @pl.when(t >= zs - 1 - z)
            def _():
                d = t - (zs - 1 - z)
                across(r, d).wait_recv()
                y[r, rows_for(d, core), :] += xbuf[d, r]

                @pl.when(z < zs - 1)
                def _():
                    leftward(r, d).wait_recv()
                    y[r, rows_for(d, core), :] += left_buf[d, r]

                @pl.when(t > zs - 1 - z)
                def _():
                    leftward(r, d - 1).wait_send()

                leftward(r, d).start()

        if t == 0:
            for r in range(rank):
                fb[j * rank + r] = factor[r, rows_of(i * n_col + j, part), :]
            for c in f_copies:
                c.wait()
            every = fb[...].reshape(total * part, LANES)
            parity = lax.broadcasted_iota(jnp.int32, every.shape, 0) & 1
            swapped = jnp.where(parity == 0, pltpu.roll(every, total * part - 1, 0), -pltpu.roll(every, 1, 0))
            sw[...] = swapped.reshape(total, part, LANES)
            lane = lax.broadcasted_iota(jnp.int32, (total, LANES), 1)
            gram = jnp.zeros((total, LANES), jnp.float32)
            for b in range(total):
                real = jnp.sum(jnp.sum(fb[...] * fb[b][None], axis=1), axis=1, keepdims=True)
                imag = jnp.sum(jnp.sum(fb[...] * sw[b][None], axis=1), axis=1, keepdims=True)
                gram = jnp.where(lane == b, real, gram)
                gram = jnp.where(lane == LANES // 2 + b, imag, gram)
            stat[8:, :] = gram
            c_copies = []
            for s in range(1, n_col):
                c_copies.append(copy(stat, stat_col.at[s], c_send.at[s], c_recv.at[s], (i, col_peer(s))))
                c_copies[-1].start()
        if t == min(1, zs - 2):
            summed = stat[...]
            for s, c in enumerate(c_copies, 1):
                c.wait()
                summed = summed + stat_col[s]
            stat_sum[...] = summed
            s_copies = []
            for s in range(1, n_set):
                s_copies.append(copy(stat_sum, stat_all.at[s], s_send.at[s], s_recv.at[s], (set_peer(s), j)))
                s_copies[-1].start()

    summed = stat_sum[...]
    for s, c in enumerate(s_copies, 1):
        c.wait()
        summed = summed + stat_all[s]
    ratio_total = jnp.sum(jnp.sum(summed[:8], axis=0, keepdims=True), axis=1, keepdims=True)
    gram = summed[8:]
    purity = jnp.sum(jnp.sum(gram * gram, axis=0, keepdims=True), axis=1, keepdims=True) / (trace_value * trace_value)
    settings_all = n_set * labels.shape[0]
    rate = (1.0 - mixing) / settings_all
    own = rate * ratio_total - 2.0 * penalty * purity
    loads[rank + 1].wait()
    for b in range(total):
        mixed = own * fb[b]
        for a in range(total):
            mixed = mixed + (2.0 * penalty / trace_value) * (
                gram[a : a + 1, b : b + 1] * fb[a]
                - gram[a : a + 1, LANES // 2 + b : LANES // 2 + b + 1] * sw[a])
        out_velocity[b] = momentum * velocity[b] + mixed

    a_copies = []
    for r in range(rank):
        across(r, z).wait_recv()
        y[r, rows_for(z, core), :] += xbuf[z, r]

        @pl.when(z > 0)
        def _():
            rightward(r, z).wait_recv()
            y[r, rows_for(z, core), :] += right_buf[z, r]

        @pl.when(z < zs - 1)
        def _():
            leftward(r, z).wait_recv()
            y[r, rows_for(z, core), :] += left_buf[z, r]

        for s in range(1, n_col):
            peer = col_peer(s)
            a_copies.append(copy(y.at[r, rows_of(i * n_col + peer, part)], ab.at[j * rank + r],
                                 a_send.at[s, r], a_recv.at[s, r], (i, peer)))
            a_copies[-1].start()
        ab[j * rank + r] = y[r, rows_of(i * n_col + j, part), :]

    for t in range(zs):
        for r in range(rank):
            across(r, lax.rem(z + t + 1, zs)).wait_send()
    for r in range(rank):
        @pl.when(z < zs - 1)
        def _():
            rightward(r, z + 1).wait_send()

        @pl.when(z > 0)
        def _():
            leftward(r, z - 1).wait_send()

    for c in a_copies:
        c.wait()
    new_velocity = out_velocity[...] - rate * ab[...]
    out_velocity[...] = new_velocity
    out_factor[...] = fb[...] - step_size * new_velocity


def interleave(x):
    n, two, m = x.shape
    return x.reshape(n, two, m // LANES, LANES).transpose(0, 2, 1, 3).reshape(n, two * m // LANES, LANES)


def separate(x):
    n, rows, lanes = x.shape
    return x.reshape(n, rows // 2, 2, lanes).transpose(0, 2, 1, 3).reshape(n, 2, rows // 2 * lanes)


def shards(n_set, n_col, factor, velocity, labels, counts):
    rank, _, order = factor.shape
    total = rank * n_col
    left, rsize = 2**QA, 2**QB
    chunk = left // n_col
    wide = 2 * order // LANES
    block = wide // n_set
    part = block // n_col
    zs = n_set // 2
    f32, bf16 = jnp.float32, jnp.bfloat16
    vmem = pl.BlockSpec(memory_space=pltpu.VMEM)
    hbm = pl.BlockSpec(memory_space=pltpu.HBM)
    dma = pltpu.SemaphoreType.DMA
    out = jax.ShapeDtypeStruct((total, part, LANES), f32)
    new_factor, new_velocity = pl.pallas_call(
        functools.partial(kernel, n_set, n_col),
        out_shape=(out, out),
        in_specs=[pl.BlockSpec(memory_space=pltpu.SMEM), hbm, hbm, hbm],
        out_specs=(vmem, vmem),
        scratch_shapes=[
            pltpu.VMEM((rank, wide, LANES), f32),
            pltpu.VMEM((total, part, LANES), f32),
            pltpu.VMEM((order // LANES, LANES), jnp.int32),
            pltpu.VMEM((rsize, rsize), bf16),
            pltpu.VMEM((2 * rank, left, rsize), bf16),
            pltpu.VMEM((2 * rank, left, rsize), bf16),
            pltpu.VMEM((2 * rank, left, rsize), f32),
            pltpu.VMEM((rank, wide, LANES), f32),
            pltpu.VMEM((n_col, chunk + 8, rsize), f32),
            pltpu.VMEM((n_col, chunk + 8, rsize), f32),
            pltpu.VMEM((chunk, rsize), f32),
            pltpu.VMEM((n_col, chunk, rsize), f32),
            pltpu.VMEM((total, part, LANES), f32),
            pltpu.VMEM((total, part, LANES), f32),
            pltpu.VMEM((total, part, LANES), f32),
            pltpu.VMEM((8 + total, LANES), f32),
            pltpu.VMEM((n_col, 8 + total, LANES), f32),
            pltpu.VMEM((8 + total, LANES), f32),
            pltpu.VMEM((n_set, 8 + total, LANES), f32),
            pltpu.VMEM((zs, rank, block, LANES), f32),
            pltpu.VMEM((zs, rank, block, LANES), f32),
            pltpu.VMEM((zs, rank, block, LANES), f32),
            dma((n_col,)), dma((n_col,)), dma((n_col,)), dma((n_col,)), dma((n_col,)), dma((n_col,)),
            dma((n_col,)), dma((n_col,)), dma((n_set,)), dma((n_set,)),
            dma((zs, rank)), dma((zs, rank)), dma((zs, rank)), dma((zs, rank)), dma((zs, rank)), dma((zs, rank)),
            dma((n_col, rank)), dma((n_col, rank)), dma((rank + 2,)),
        ],
        compiler_params=pltpu.CompilerParams(
            collective_id=0, has_side_effects=True, vmem_limit_bytes=55888896),
        name="tomography_step",
    )(labels, interleave(factor), interleave(velocity), counts.reshape(order // LANES, LANES))
    return separate(new_factor), separate(new_velocity)


def solution(mesh):
    in_specs = (P("col", None, None), P(None, None, ("set", "col")), P("set", None), P("set", None))
    out_specs = (P(None, None, ("set", "col")), P(None, None, ("set", "col")))
    body = functools.partial(shards, mesh.shape["set"], mesh.shape["col"])
    return jax.shard_map(body, mesh=mesh, in_specs=in_specs, out_specs=out_specs, check_vma=False)
```

```python
import functools

import jax
import jax.numpy as jnp
from jax import lax
from jax.experimental import pallas as pl
from jax.experimental.pallas import tpu as pltpu
from jax.sharding import PartitionSpec as P

QA = 8
QB = 9
LANES = 128

mixing = 0.1
penalty = 8.0
momentum = 0.9
step_size = 0.5
count_norm = 8.0
MESH = pl.DeviceIdType.MESH


def fold_parity(x):
    x = x ^ (x >> 8)
    x = x ^ (x >> 4)
    x = x ^ (x >> 2)
    x = x ^ (x >> 1)
    return x & 1


def bit_count(x):
    x = x - ((x >> 1) & 0x55555)
    x = (x & 0x33333) + ((x >> 2) & 0x33333)
    x = (x + (x >> 4)) & 0xF0F0F
    return (x + (x >> 8) + (x >> 16)) & 0xFF


def sign_matrix(mask, size):
    row = lax.broadcasted_iota(jnp.int32, (size, size), 0)
    col = lax.broadcasted_iota(jnp.int32, (size, size), 1)
    sign = 1 - 2 * fold_parity(row & col & mask)
    keep = ((row ^ col) & (mask ^ (size - 1))) == 0
    return jnp.where(keep, sign, 0).astype(jnp.float32).astype(jnp.bfloat16)


def split(x):
    high = x.astype(jnp.bfloat16)
    return high, (x - high.astype(jnp.float32)).astype(jnp.bfloat16)


def dot(a, b):
    return jnp.dot(a, b, preferred_element_type=jnp.float32)


def kernel(n_set, n_col, labels, factor_hbm, velocity_hbm, counts_hbm, out_factor, out_velocity,
           factor, velocity, counts, hb, high, low, g, y, psend, precv, wown, wrecv, fb, sw, ab, stat, stat_col, stat_sum, stat_all,
           xbuf, right_buf, left_buf,
           f_send, f_recv, p_send, p_recv, w_send, w_recv, c_send, c_recv, s_send, s_recv,
           x_send, x_recv, r_send, r_recv, l_send, l_recv, a_send, a_recv, load_sem):
    rank = factor.shape[0]
    left, rsize = 2**QA, 2**QB
    order = left * rsize
    tiles = rsize // LANES
    total = n_col * rank
    chunk = left // n_col
    block = factor.shape[1] // n_set
    part = block // n_col
    zs = n_set // 2
    i = lax.axis_index("set")
    j = lax.axis_index("col")
    z, core = i // 2, i % 2

    def col_peer(s):
        return lax.rem(j + s, n_col)

    def set_peer(s):
        return lax.rem(i + s, n_set)

    def rows_of(index, size):
        return pl.ds(pl.multiple_of(index * size, size), size)

    loads = [pltpu.make_async_copy(factor_hbm.at[r], factor.at[r], load_sem.at[r]) for r in range(rank)]
    loads.append(pltpu.make_async_copy(counts_hbm, counts, load_sem.at[rank]))
    loads.append(pltpu.make_async_copy(velocity_hbm, velocity, load_sem.at[rank + 1]))
    for load in loads:
        load.start()
    barrier = pltpu.get_barrier_semaphore()
    for s in range(1, n_col):
        pl.semaphore_signal(barrier, inc=1, device_id=(i, col_peer(s)), device_id_type=MESH)
    for s in range(1, n_set):
        pl.semaphore_signal(barrier, inc=1, device_id=(set_peer(s), j), device_id_type=MESH)

    def copy(src, dst, send, recv, where):
        return pltpu.make_async_remote_copy(
            src_ref=src, dst_ref=dst, send_sem=send, recv_sem=recv, device_id=where, device_id_type=MESH)

    nonz = jnp.int32(0)
    ymask = jnp.int32(0)
    scale = jnp.float32(1.0)
    for q in range(QA + QB):
        label = labels[0, q]
        bit = 1 << (QA + QB - 1 - q)
        nonz = nonz + jnp.where(label == 2, 0, bit)
        ymask = ymask + jnp.where(label == 1, bit, 0)
        scale = scale * jnp.where(label == 2, 1.0, 0.5).astype(jnp.float32)
    ha = sign_matrix(nonz >> QB, left)
    hb[...] = sign_matrix(nonz & (rsize - 1), rsize)

    index = (lax.broadcasted_iota(jnp.int32, (left, LANES), 0) * rsize
             + lax.broadcasted_iota(jnp.int32, (left, LANES), 1))

    def phases(b):
        phase = bit_count((index + b * LANES) & ymask) & 3
        odd = (phase & 1) == 1
        late = (1 - 2 * (phase >> 1)).astype(jnp.float32)
        mid = (1 - 2 * ((phase ^ (phase >> 1)) & 1)).astype(jnp.float32)
        return odd, late, mid

    for load in loads[:rank]:
        load.wait()
    square = jnp.zeros((left, LANES), jnp.float32)
    for b in range(tiles):
        odd, late, mid = phases(b)
        lanes = slice(b * LANES, (b + 1) * LANES)
        for r in range(rank):
            re = factor[r, pl.ds(2 * b, left, stride=2 * tiles), :]
            im = factor[r, pl.ds(2 * b + 1, left, stride=2 * tiles), :]
            square = square + re * re + im * im
            for c, x in enumerate((jnp.where(odd, im, re) * late, jnp.where(odd, re, im) * mid)):
                xh, xl = split(x)
                high[2 * r + c, :, lanes] = xh
                low[2 * r + c, :, lanes] = xl
    for rc in range(2 * rank):
        first = dot(ha, high[rc]) + dot(ha, low[rc])
        xh, xl = split(first)
        high[rc] = xh
        low[rc] = xl
    pl.semaphore_wait(barrier, n_col - 1 + n_set - 1)
    trace_part = jnp.sum(jnp.sum(square, axis=0, keepdims=True), axis=1, keepdims=True)

    p_copies = []
    for s in list(range(1, n_col)) + [0]:
        peer = col_peer(s)
        rows = rows_of(peer, chunk)
        xh = high[:, rows, :].reshape(2 * rank * chunk, rsize)
        xl = low[:, rows, :].reshape(2 * rank * chunk, rsize)
        second = (dot(xh, hb[...]) + dot(xl, hb[...])).reshape(2 * rank, chunk, rsize)
        g[:, rows, :] = second
        psend[s, :chunk, :] = scale * jnp.sum(second * second, axis=0)
        psend[s, chunk:, :] = jnp.broadcast_to(trace_part, (8, rsize))
        if s:
            p_copies.append(copy(psend.at[s], precv.at[s], p_send.at[s], p_recv.at[s], (i, peer)))
            p_copies[-1].start()

    loads[rank].wait()
    count = jnp.concatenate(
        [counts[pl.ds(j * (chunk * tiles) + b, chunk, stride=tiles), :] for b in range(tiles)], axis=1
    ).astype(jnp.float32)
    prob = psend[0]
    for s, c in enumerate(p_copies, 1):
        c.wait()
        prob = prob + precv[s]
    trace_value = prob[chunk : chunk + 1, :1]
    prob = prob[:chunk]
    quasi = (1.0 - mixing) * prob / trace_value + mixing / order
    weight = count / (count_norm * order * quasi)
    wown[...] = weight
    w_copies = []
    for s in range(1, n_col):
        w_copies.append(copy(wown, wrecv.at[s], w_send.at[s], w_recv.at[s], (i, col_peer(s))))
        w_copies[-1].start()
    ratio = jnp.sum((weight * prob / trace_value).reshape(chunk // 8, 8, rsize), axis=0)
    folded = ratio[:, :LANES]
    for b in range(1, tiles):
        folded = folded + ratio[:, b * LANES : (b + 1) * LANES]
    stat[:8, :] = folded

    odd_late_mid = [phases(b) for b in range(tiles)]
    for s in range(n_col):
        if s:
            w_copies[s - 1].wait()
            weight = wrecv[s]
        else:
            weight = wown[...]
        rows = rows_of(lax.rem(j - s + n_col, n_col), chunk)
        xh, xl = split((g[:, rows, :] * (weight * scale)[None]).reshape(2 * rank * chunk, rsize))
        xh, xl = split(dot(xh, hb[...]) + dot(xl, hb[...]))
        high[:, rows, :] = xh.reshape(2 * rank, chunk, rsize)
        low[:, rows, :] = xl.reshape(2 * rank, chunk, rsize)

    mine = pl.ds(j * rank, rank)
    f_copies = []
    for s in range(1, n_col):
        peer = col_peer(s)
        f_copies.append(copy(factor.at[:, rows_of(i * n_col + peer, part)], fb.at[mine],
                             f_send.at[s], f_recv.at[s], (i, peer)))
        f_copies[-1].start()

    def rows_for(d, side):
        return rows_of(2 * d + side, block)

    def across(r, d):
        return copy(y.at[r, rows_for(d, 1 - core)], xbuf.at[d, r], x_send.at[d, r], x_recv.at[d, r],
                    (2 * z + 1 - core, j))

    def rightward(r, d):
        return copy(y.at[r, rows_for(d, core)], right_buf.at[d, r], r_send.at[d, r], r_recv.at[d, r],
                    (lax.rem(i + 2, n_set), j))

    def leftward(r, d):
        return copy(y.at[r, rows_for(d, core)], left_buf.at[d, r], l_send.at[d, r], l_recv.at[d, r],
                    (lax.rem(i + n_set - 2, n_set), j))

    for r in range(rank):
        re_all = dot(ha, high[2 * r]) + dot(ha, low[2 * r])
        im_all = dot(ha, high[2 * r + 1]) + dot(ha, low[2 * r + 1])
        for b in range(tiles):
            odd, late, mid = odd_late_mid[b]
            re = re_all[:, b * LANES : (b + 1) * LANES]
            im = im_all[:, b * LANES : (b + 1) * LANES]
            y[r, pl.ds(2 * b, left, stride=2 * tiles), :] = jnp.where(odd, im, re) * mid
            y[r, pl.ds(2 * b + 1, left, stride=2 * tiles), :] = jnp.where(odd, re, im) * late
        for t in range(zs - 1):
            @pl.when(t >= z)
            def _():
                across(r, z + zs - 1 - t).start()

            @pl.when(t >= zs - 1 - z)
            def _():
                across(r, t - (zs - 1 - z)).start()
        across(r, z).start()

    for t in range(zs - 1):
        for r in range(rank):
            @pl.when(t >= z)
            def _():
                d = z + zs - 1 - t
                across(r, d).wait_recv()
                y[r, rows_for(d, core), :] += xbuf[d, r]

                @pl.when(z > 0)
                def _():
                    rightward(r, d).wait_recv()
                    y[r, rows_for(d, core), :] += right_buf[d, r]

                @pl.when(t > z)
                def _():
                    rightward(r, d + 1).wait_send()

                rightward(r, d).start()

            @pl.when(t >= zs - 1 - z)
            def _():
                d = t - (zs - 1 - z)
                across(r, d).wait_recv()
                y[r, rows_for(d, core), :] += xbuf[d, r]

                @pl.when(z < zs - 1)
                def _():
                    leftward(r, d).wait_recv()
                    y[r, rows_for(d, core), :] += left_buf[d, r]

                @pl.when(t > zs - 1 - z)
                def _():
                    leftward(r, d - 1).wait_send()

                leftward(r, d).start()

        if t == 0:
            for r in range(rank):
                fb[j * rank + r] = factor[r, rows_of(i * n_col + j, part), :]
            for c in f_copies:
                c.wait()
            every = fb[...].reshape(total * part, LANES)
            parity = lax.broadcasted_iota(jnp.int32, every.shape, 0) & 1
            swapped = jnp.where(parity == 0, pltpu.roll(every, total * part - 1, 0), -pltpu.roll(every, 1, 0))
            sw[...] = swapped.reshape(total, part, LANES)
            lane = lax.broadcasted_iota(jnp.int32, (total, LANES), 1)
            gram = jnp.zeros((total, LANES), jnp.float32)
            for b in range(total):
                real = jnp.sum(jnp.sum(fb[...] * fb[b][None], axis=1), axis=1, keepdims=True)
                imag = jnp.sum(jnp.sum(fb[...] * sw[b][None], axis=1), axis=1, keepdims=True)
                gram = jnp.where(lane == b, real, gram)
                gram = jnp.where(lane == LANES // 2 + b, imag, gram)
            stat[8:, :] = gram
            c_copies = []
            for s in range(1, n_col):
                c_copies.append(copy(stat, stat_col.at[s], c_send.at[s], c_recv.at[s], (i, col_peer(s))))
                c_copies[-1].start()
        if t == min(1, zs - 2):
            summed = stat[...]
            for s, c in enumerate(c_copies, 1):
                c.wait()
                summed = summed + stat_col[s]
            stat_sum[...] = summed
            s_copies = []
            for s in range(1, n_set):
                s_copies.append(copy(stat_sum, stat_all.at[s], s_send.at[s], s_recv.at[s], (set_peer(s), j)))
                s_copies[-1].start()

    summed = stat_sum[...]
    for s, c in enumerate(s_copies, 1):
        c.wait()
        summed = summed + stat_all[s]
    ratio_total = jnp.sum(jnp.sum(summed[:8], axis=0, keepdims=True), axis=1, keepdims=True)
    gram = summed[8:]
    purity = jnp.sum(jnp.sum(gram * gram, axis=0, keepdims=True), axis=1, keepdims=True) / (trace_value * trace_value)
    settings_all = n_set * labels.shape[0]
    rate = (1.0 - mixing) / settings_all
    own = rate * ratio_total - 2.0 * penalty * purity
    loads[rank + 1].wait()
    for b in range(total):
        mixed = own * fb[b]
        for a in range(total):
            mixed = mixed + (2.0 * penalty / trace_value) * (
                gram[a : a + 1, b : b + 1] * fb[a]
                - gram[a : a + 1, LANES // 2 + b : LANES // 2 + b + 1] * sw[a])
        out_velocity[b] = momentum * velocity[b] + mixed

    a_copies = []
    for r in range(rank):
        across(r, z).wait_recv()
        y[r, rows_for(z, core), :] += xbuf[z, r]

        @pl.when(z > 0)
        def _():
            rightward(r, z).wait_recv()
            y[r, rows_for(z, core), :] += right_buf[z, r]

        @pl.when(z < zs - 1)
        def _():
            leftward(r, z).wait_recv()
            y[r, rows_for(z, core), :] += left_buf[z, r]

        for s in range(1, n_col):
            peer = col_peer(s)
            a_copies.append(copy(y.at[r, rows_of(i * n_col + peer, part)], ab.at[j * rank + r],
                                 a_send.at[s, r], a_recv.at[s, r], (i, peer)))
            a_copies[-1].start()
        ab[j * rank + r] = y[r, rows_of(i * n_col + j, part), :]

    for t in range(zs):
        for r in range(rank):
            across(r, lax.rem(z + t + 1, zs)).wait_send()
    for r in range(rank):
        @pl.when(z < zs - 1)
        def _():
            rightward(r, z + 1).wait_send()

        @pl.when(z > 0)
        def _():
            leftward(r, z - 1).wait_send()

    for c in a_copies:
        c.wait()
    new_velocity = out_velocity[...] - rate * ab[...]
    out_velocity[...] = new_velocity
    out_factor[...] = fb[...] - step_size * new_velocity


def interleave(x):
    n, two, m = x.shape
    return x.reshape(n, two, m // LANES, LANES).transpose(0, 2, 1, 3).reshape(n, two * m // LANES, LANES)


def separate(x):
    n, rows, lanes = x.shape
    return x.reshape(n, rows // 2, 2, lanes).transpose(0, 2, 1, 3).reshape(n, 2, rows // 2 * lanes)


def shards(n_set, n_col, factor, velocity, labels, counts):
    rank, _, order = factor.shape
    total = rank * n_col
    left, rsize = 2**QA, 2**QB
    chunk = left // n_col
    wide = 2 * order // LANES
    block = wide // n_set
    part = block // n_col
    zs = n_set // 2
    f32, bf16 = jnp.float32, jnp.bfloat16
    vmem = pl.BlockSpec(memory_space=pltpu.VMEM)
    hbm = pl.BlockSpec(memory_space=pltpu.HBM)
    dma = pltpu.SemaphoreType.DMA
    out = jax.ShapeDtypeStruct((total, part, LANES), f32)
    new_factor, new_velocity = pl.pallas_call(
        functools.partial(kernel, n_set, n_col),
        out_shape=(out, out),
        in_specs=[pl.BlockSpec(memory_space=pltpu.SMEM), hbm, hbm, hbm],
        out_specs=(vmem, vmem),
        scratch_shapes=[
            pltpu.VMEM((rank, wide, LANES), f32),
            pltpu.VMEM((total, part, LANES), f32),
            pltpu.VMEM((order // LANES, LANES), jnp.int32),
            pltpu.VMEM((rsize, rsize), bf16),
            pltpu.VMEM((2 * rank, left, rsize), bf16),
            pltpu.VMEM((2 * rank, left, rsize), bf16),
            pltpu.VMEM((2 * rank, left, rsize), f32),
            pltpu.VMEM((rank, wide, LANES), f32),
            pltpu.VMEM((n_col, chunk + 8, rsize), f32),
            pltpu.VMEM((n_col, chunk + 8, rsize), f32),
            pltpu.VMEM((chunk, rsize), f32),
            pltpu.VMEM((n_col, chunk, rsize), f32),
            pltpu.VMEM((total, part, LANES), f32),
            pltpu.VMEM((total, part, LANES), f32),
            pltpu.VMEM((total, part, LANES), f32),
            pltpu.VMEM((8 + total, LANES), f32),
            pltpu.VMEM((n_col, 8 + total, LANES), f32),
            pltpu.VMEM((8 + total, LANES), f32),
            pltpu.VMEM((n_set, 8 + total, LANES), f32),
            pltpu.VMEM((zs, rank, block, LANES), f32),
            pltpu.VMEM((zs, rank, block, LANES), f32),
            pltpu.VMEM((zs, rank, block, LANES), f32),
            dma((n_col,)), dma((n_col,)), dma((n_col,)), dma((n_col,)), dma((n_col,)), dma((n_col,)),
            dma((n_col,)), dma((n_col,)), dma((n_set,)), dma((n_set,)),
            dma((zs, rank)), dma((zs, rank)), dma((zs, rank)), dma((zs, rank)), dma((zs, rank)), dma((zs, rank)),
            dma((n_col, rank)), dma((n_col, rank)), dma((rank + 2,)),
        ],
        compiler_params=pltpu.CompilerParams(
            collective_id=0, has_side_effects=True, vmem_limit_bytes=55888896),
        name="tomography_step",
    )(labels, interleave(factor), interleave(velocity), counts.reshape(order // LANES, LANES))
    return separate(new_factor), separate(new_velocity)


def solution(mesh):
    in_specs = (P("col", None, None), P(None, None, ("set", "col")), P("set", None), P("set", None))
    out_specs = (P(None, None, ("set", "col")), P(None, None, ("set", "col")))
    body = functools.partial(shards, mesh.shape["set"], mesh.shape["col"])
    return jax.shard_map(body, mesh=mesh, in_specs=in_specs, out_specs=out_specs, check_vma=False)
```
